32 devices in a mesh: seq: 8 (over z, y), head: 4 (over x, core).
Axes of the slice: x: 2, y: 2, z: 4, core: 2. Of those that a mesh axis runs over, the one named last changes fastest.
Arguments:
- inputs: bfloat16 [2048, 2048], P('seq', 'head'), may hold values from -6 to 6
- w_query: bfloat16 [2048, 2048], P(None, 'head'), may hold values from -0.125 to 0.125
- w_key: bfloat16 [2048, 2048], P(None, 'head'), may hold values from -0.125 to 0.125
- w_value: bfloat16 [2048, 2048], P(None, 'head'), may hold values from -0.125 to 0.125
- sketch: float32 [2, 64, 32], replicated, may hold values from -0.75 to 0.75
- prefix_state: float32 [32, 1024, 64], P('head'), may hold values from -56 to 56
- prefix_norm: float32 [32, 1024], P('head'), as said below
- d_attn: bfloat16 [2048, 2048], P('seq', 'head'), may hold values from -128 to 128
- d_state_end: float32 [32, 1024, 64], P('head'), may hold values from -6 to 6
- d_norm_end: float32 [32, 1024], P('head'), may hold values from -4 to 4
Outputs:
- d_input: bfloat16 [2048, 2048], P('seq', 'head')
- d_query: bfloat16 [2048, 2048], P('seq', 'head')
- d_key: bfloat16 [2048, 2048], P('seq', 'head')
- d_value: bfloat16 [2048, 2048], P('seq', 'head')
- d_prefix_state: float32 [32, 1024, 64], P('head')
- d_prefix_norm: float32 [32, 1024], P('head')
The draws below stay inside these ranges and needn't reach their ends.
Inputs may be any that keep to these rules, and one draw needn't show every extreme that they name: For every head, prefix_norm laid out as a 32 x 32 matrix is symmetric positive semidefinite.
All inputs are finite; a program needn't handle non-finite values.
Results may differ from the reference program's by a relative error of at most 0.012.
Values may be sent and summed in bfloat16 or wider, within the bound.
No kernel may reach another device: no remote copies, remote signals or barrier semaphores. Data moves between devices by JAX's collectives and lax.ppermute only.
A program may use at most 192 MiB of HBM per device.

```python
from functools import partial
import jax
import jax.numpy as jnp
from jax import lax

D = 2048
HEADS = 32
HD = 64
SK = 32
FEAT = 1024
TOK_DEV = 256
TOKENS = 2048


def draw_prefix_norm(key, part):
    points = jax.random.normal(jax.random.fold_in(key, 11), (HEADS, 64, SK), jnp.float32) * SK ** (-0.5)
    gram = jnp.einsum('hmi,hmj->hij', points, points) * (TOKENS / 64.0)
    return gram.reshape(HEADS, SK * SK).astype(jnp.float32)


def block_levels(stream_key, shape, shards, low, top_value):
    def one(dim, parts):
        draws = jax.random.uniform(jax.random.fold_in(jax.random.fold_in(stream_key, 6), dim), (parts,), jnp.float32, low / len(shards), top_value / len(shards))
        return jnp.repeat(jnp.exp(draws), shape[dim] // parts).reshape((-1,) + (1,) * (len(shape) - dim - 1))

    factor_of = one(*shards[0])
    for cut in shards[1:]:
        factor_of = factor_of * one(*cut)
    return factor_of


def normal_values(own_key, dims, deviation, bound, cuts=(), kind=jnp.bfloat16):
    level = block_levels(own_key, dims, cuts, -0.22, 0.18) if cuts else 1.0
    drawn = jax.random.normal(own_key, dims, jnp.float32) * deviation * level
    return jnp.minimum(jnp.maximum(drawn, -bound), bound).astype(kind)


def setup_inputs(seed: int = 0) -> dict:
    key_list = jax.random.split(jax.random.key(seed), 11)
    return {
        "inputs": normal_values(key_list[0], (TOKENS, D), 1.0, 6.0, ((0, 8), (1, 4))),
        "w_query": normal_values(key_list[1], (D, HEADS * HD), D ** -0.5, 0.125, ((1, 4),)),
        "w_key": normal_values(key_list[2], (D, HEADS * HD), D ** -0.5, 0.125, ((1, 4),)),
        "w_value": normal_values(key_list[3], (D, HEADS * HD), D ** -0.5, 0.125, ((1, 4),)),
        "sketch": normal_values(key_list[4], (2, HD, SK), HD ** -0.5, 0.75, (), jnp.float32),
        "prefix_state": normal_values(key_list[5], (HEADS, FEAT, HD), (0.2 * TOKENS ** 0.5), 56.0, ((0, 4),), jnp.float32),
        "prefix_norm": draw_prefix_norm(jax.random.fold_in(key_list[10], 71), 0),
        "d_attn": normal_values(key_list[7], (TOKENS, HEADS * HD), (0.5 * TOKENS ** 0.5), 128.0, ((0, 8), (1, 4))),
        "d_state_end": normal_values(key_list[8], (HEADS, FEAT, HD), 1.0, 6.0, ((0, 4),), jnp.float32),
        "d_norm_end": normal_values(key_list[9], (HEADS, FEAT), 0.3, 4.0, ((0, 4),), jnp.float32),
    }


HIGHEST_PRECISION = lax.Precision.HIGHEST

def sketch_map(values, sketch):
    left_map = jnp.einsum('hbd,de->hbe', values, sketch[0], precision=HIGHEST_PRECISION)
    right_map = jnp.einsum('hbd,de->hbe', values, sketch[1], precision=HIGHEST_PRECISION)
    return left_map * right_map * sketch.shape[2] ** (-0.5)

def square_features(sketched):
    outer_prod = sketched[:, :, :, None] * sketched[:, :, None, :]
    return outer_prod.reshape(sketched.shape[0], sketched.shape[1], -1)

def attend_block(carried, block_data, sketch):
    value_state, norm_state = carried
    query_block, key_block, value_block = block_data
    sketch_query = sketch_map(query_block, sketch)
    sketch_key = sketch_map(key_block, sketch)
    feat_query = square_features(sketch_query)
    feat_key = square_features(sketch_key)
    block_size = query_block.shape[1]
    causal = lax.broadcasted_iota(jnp.int32, (block_size, block_size), 0) >= lax.broadcasted_iota(jnp.int32, (block_size, block_size), 1)
    dot_prod = jnp.einsum('hid,hjd->hij', sketch_query, sketch_key, precision=HIGHEST_PRECISION)
    scores = jnp.where(causal, dot_prod * dot_prod, jnp.zeros_like(dot_prod))
    numerator = jnp.einsum('hif,hfd->hid', feat_query, value_state, precision=HIGHEST_PRECISION)
    numerator = numerator + jnp.einsum('hij,hjd->hid', scores, value_block, precision=HIGHEST_PRECISION)
    denominator = 1.0 + jnp.einsum('hif,hf->hi', feat_query, norm_state, precision=HIGHEST_PRECISION) + scores.sum(-1)
    outputs = numerator / denominator[:, :, None]
    value_state = value_state + jnp.einsum('hjf,hjd->hfd', feat_key, value_block, precision=HIGHEST_PRECISION)
    norm_state = norm_state + feat_key.sum(1)
    return ((value_state, norm_state), outputs)

def split_blocks(values, block_size):
    head_count, total_rows, depth_size = values.shape
    return values.reshape(head_count, total_rows // block_size, block_size, depth_size).transpose(1, 0, 2, 3)

def join_blocks(values):
    block_count, head_count, block_size, depth_size = values.shape
    return values.transpose(1, 0, 2, 3).reshape(head_count, block_count * block_size, depth_size)

def attend(query, key, value, value_state, norm_state, sketch):
    block_size = min(TOK_DEV, 512)
    block_step = jax.checkpoint(partial(attend_block, sketch=sketch))
    carried, outputs = lax.scan(block_step, (value_state, norm_state), (split_blocks(query, block_size), split_blocks(key, block_size), split_blocks(value, block_size)))
    return (join_blocks(outputs), carried[0], carried[1])

def reference(inputs, w_query, w_key, w_value, sketch, prefix_state, prefix_norm, d_attn, d_state_end, d_norm_end):

    def to_heads(values):
        return values.reshape(TOKENS, HEADS, HD).transpose(1, 0, 2).astype(jnp.float32)

    def flatten(values):
        return values.transpose(1, 0, 2).reshape(TOKENS, HEADS * HD).astype(jnp.bfloat16)
    query = to_heads(lax.optimization_barrier(jnp.dot(inputs, w_query, preferred_element_type=jnp.float32).astype(jnp.bfloat16)))
    key = to_heads(lax.optimization_barrier(jnp.dot(inputs, w_key, preferred_element_type=jnp.float32).astype(jnp.bfloat16)))
    value = to_heads(lax.optimization_barrier(jnp.dot(inputs, w_value, preferred_element_type=jnp.float32).astype(jnp.bfloat16)))

    def forward(query_in, key_in, value_in, state_in, norm_in):
        return attend(query_in, key_in, value_in, state_in, norm_in, sketch)
    primal, pull_back = jax.vjp(forward, query, key, value, prefix_state, prefix_norm)
    grad_query, grad_key, grad_value, grad_state, grad_norm = pull_back((to_heads(d_attn), d_state_end, d_norm_end))
    d_query = flatten(grad_query)
    d_key = flatten(grad_key)
    d_value = flatten(grad_value)
    d_input = jnp.dot(d_query, w_query.T, preferred_element_type=jnp.float32)
    d_input = d_input + jnp.dot(d_key, w_key.T, preferred_element_type=jnp.float32)
    d_input = d_input + jnp.dot(d_value, w_value.T, preferred_element_type=jnp.float32)
    return (d_input.astype(jnp.bfloat16), d_query, d_key, d_value, grad_state, grad_norm)
```

```python
import math
from functools import partial

import jax
import jax.numpy as jnp
import numpy as np
from jax import lax
from jax.experimental import pallas as pl
from jax.experimental.pallas import tpu as pltpu
from jax.sharding import Mesh, PartitionSpec as P

F32 = jnp.float32
BF16 = jnp.bfloat16
LANES = 128
VMEM = pltpu.VMEM
MIB = 1024 * 1024

NN = (((1,), (0,)), ((), ()))
NT = (((1,), (1,)), ((), ()))
TN = (((0,), (0,)), ((), ()))


def mm(a, b, dims=NN):
    return lax.dot_general(a, b, dims, preferred_element_type=F32)


def split(x):
    hi = x.astype(BF16)
    return hi, (x - hi.astype(F32)).astype(BF16)


def tile_count(sk):
    return -(-(sk // 2 + 1) // (LANES // sk))


def pair_map(sk):
    step = LANES // sk
    width = tile_count(sk) * LANES
    lane = np.arange(width)
    tile, within = lane // LANES, lane % LANES
    j, a = within // sk, within % sk
    first, second = (a + j) % sk, (a - step * tile) % sk
    keep = step * tile + j <= sk // 2
    table = np.zeros((sk * sk, width), np.float32)
    for one in lane[keep]:
        x, y = first[one], second[one]
        r = step * tile[one] + j[one]
        if r == 0:
            table[x * sk + y, one] = 1.0
        else:
            value = 0.5 if 2 * r == sk else 1.0
            table[x * sk + y, one] = value
            table[y * sk + x, one] = value
    return table


def lane_weights(sk, width):
    lane = lax.broadcasted_iota(jnp.int32, (1, width), 1)
    r = (LANES // sk) * (lane // LANES) + (lane % LANES) // sk
    return jnp.where(
        r <= sk // 2, jnp.where((r == 0) | (2 * r == sk), 1.0, 2.0), 0.0
    ).astype(F32)


def sketched(x, weights):
    both = mm(jnp.concatenate([x, x], axis=1), weights)
    return tuple(both[:, LANES * i : LANES * (i + 1)] for i in range(4))


def turned(e, sk, tiles):
    step = LANES // sk
    return [e] + [pltpu.roll(e, step * t, 1) for t in range(1, tiles)]


def features(e, d, sk, tiles):
    return jnp.concatenate([(d * x).astype(BF16) for x in turned(e, sk, tiles)], axis=1)


def feature_pull(cot, e, d, sk, tiles):
    step = LANES // sk
    cot_e = cot_d = None
    for t, x in enumerate(turned(e, sk, tiles)):
        part = cot[:, LANES * t : LANES * (t + 1)]
        to_d = part * x
        to_e = part * d
        if t:
            to_e = pltpu.roll(to_e, LANES - step * t, 1)
        cot_d = to_d if cot_d is None else cot_d + to_d
        cot_e = to_e if cot_e is None else cot_e + to_e
    return cot_e, cot_d


def lane_of(rows):
    return lax.broadcasted_iota(jnp.int32, (rows, LANES), 1)


def base_kernel(sk, start_ref, state_ref, norm_ref, dstate_ref, dnorm_ref, map_ref, fwd_ref, bwd_ref, rows_ref):
    table = map_ref[...]
    half = state_ref.shape[1]

    def mapped(x):
        hi, lo = split(x)
        return mm(hi, table) + mm(lo, table)

    row = start_ref[0] + pl.program_id(0)
    for which, (s_ref, n_ref, o_ref, scale) in enumerate(
        ((state_ref, norm_ref, fwd_ref, 1.0), (dstate_ref, dnorm_ref, bwd_ref, 1.0 / half))
    ):
        rows_ref[which] = mapped(n_ref[...]) * scale
        o_ref[0, :half] = mapped(s_ref[0])
        o_ref[0, half:] = jnp.broadcast_to(
            rows_ref[which, pl.ds(row, 1), :], (LANES - half, o_ref.shape[2])
        )


def project_kernel(hd, count, where_ref, *refs):
    pieces = refs[:count]
    weights = refs[count:-1]
    out = refs[-1]
    depth = pieces[0].shape[1]
    sums = []
    for w in weights:
        total = None
        for i, x in enumerate(pieces):
            rows = pl.ds(pl.multiple_of(where_ref[i] * depth, depth), depth)
            part = mm(x[...], w[rows, :])
            total = part if total is None else total + part
        sums.append(total)
    heads = out.shape[0]
    if len(sums) == 2:
        for h in range(heads):
            cols = slice(h * hd, (h + 1) * hd)
            out[h] = jnp.concatenate([sums[0][:, cols], sums[1][:, cols]], axis=1).astype(BF16)
    else:
        half = out.shape[1]
        for h in range(heads):
            cols = slice(h * hd, (h + 1) * hd)
            out[h] = jnp.concatenate(
                [sums[0][:half, cols], sums[0][half:, cols]], axis=1
            ).astype(BF16)


def key_kernel(sk, hd, vk_ref, base_ref, wb_ref, state_ref, feat_ref, kdot_ref, total_ref):
    blocks, _, rows, _ = vk_ref.shape
    width = base_ref.shape[2]
    tiles = width // LANES
    weights = lane_weights(sk, width)
    lane = lane_of(rows)
    state = base_ref[0]
    for c in range(blocks):
        state_ref[0, c] = state.astype(BF16)
        vk = vk_ref[c, 0]
        e0, e1, d0, d1 = sketched(vk, wb_ref[...])
        e, d = e0 * e1, d0 * d1
        feat = features(e, d, sk, tiles)
        feat_ref[0, c] = feat
        hi, lo = split(e)
        kdot_ref[0, c] = jnp.where(
            lane < 2 * sk, hi.astype(F32), jnp.where(lane < 3 * sk, lo.astype(F32), 0.0)
        ).astype(BF16)
        ones = jnp.where(lane < hd, vk.astype(F32), 1.0).astype(BF16)
        state = state + mm(ones, feat, TN) * weights
    total_ref[0] = state


def query_kernel(
    sk, hd, q_ref, g_ref, vk_ref, kdot_ref, state_ref, wa_ref, wb_ref, ba_ref, bb_ref,
    dq_ref, qdot_ref, dn_ref, cot_ref, total_ref,
):
    blocks, _, rows, _ = vk_ref.shape
    half = rows // 2
    width = state_ref.shape[3]
    tiles = width // LANES
    lane = lane_of(rows)
    low = lane < hd
    causal = lax.broadcasted_iota(jnp.int32, (rows, rows), 0) >= lax.broadcasted_iota(
        jnp.int32, (rows, rows), 1
    )
    r_i = lax.broadcasted_iota(jnp.int32, (2 * LANES, LANES), 0) % LANES
    c_i = lax.broadcasted_iota(jnp.int32, (2 * LANES, LANES), 1)
    adder = jnp.where((r_i < hd) & (c_i >= hd), -1.0 / (LANES - hd), 0.0).astype(BF16)
    total = jnp.zeros((LANES, width), F32)
    for c in range(blocks):
        q = q_ref[c, 0]
        top = sketched(q, wa_ref[...])
        bottom = sketched(q, wb_ref[...])
        e0, e1, d0, d1 = tuple(jnp.concatenate([a, b], axis=0) for a, b in zip(top, bottom))
        e, d = e0 * e1, d0 * d1
        feat = features(e, d, sk, tiles)
        hi, lo = split(e)
        qdot = jnp.where(
            (lane >= sk) & (lane < 2 * sk), lo.astype(F32), jnp.where(lane < 3 * sk, hi.astype(F32), 0.0)
        ).astype(BF16)
        qdot_ref[0, c] = qdot
        kdot = kdot_ref[0, c]
        state = state_ref[0, c]
        ones = jnp.where(low, vk_ref[c, 0].astype(F32), 1.0).astype(BF16)
        dots = jnp.where(causal, mm(qdot, kdot, NT), 0.0)
        num = mm(feat, state, NT) + mm((dots * dots).astype(BF16), ones)
        inv = 1.0 / (1.0 + num)
        inv = jnp.where(low, pltpu.roll(inv, hd, 1), inv)
        g = g_ref[c, 0].astype(F32)
        g = jnp.concatenate([g, pltpu.roll(g, hd, 1)], axis=0)
        g_hi, g_lo = split(jnp.where(low, g * num, 0.0))
        den = mm(jnp.concatenate([g_hi, g_lo], axis=1), adder)
        dn = (jnp.where(low, g, den * inv) * inv).astype(BF16)
        dn_ref[0, c] = dn
        cot_dots = (2.0 * dots * mm(dn, ones, NT)).astype(BF16)
        near = mm(cot_dots, kdot)
        cot = mm(dn, state)
        cot_e, cot_d = feature_pull(cot, e, d, sk, tiles)
        cot_e = cot_e + jnp.where((lane < sk) | (lane >= 2 * sk), near, 0.0)
        back = jnp.concatenate(
            [(cot_e * e1).astype(BF16), (cot_e * e0).astype(BF16), (cot_d * d1).astype(BF16), (cot_d * d0).astype(BF16)],
            axis=1,
        )
        dq_ref[c, 0] = (mm(back[:half], ba_ref[...]) + mm(back[half:], bb_ref[...])).astype(BF16)
        here = mm(dn, feat, TN)
        cot_ref[0, c] = here
        total = total + here
    total_ref[0] = total[: total_ref.shape[1]].astype(BF16)


def reverse_kernel(
    sk, hd, vk_ref, feat_ref, kdot_ref, qdot_ref, dn_ref, cot_ref, base_ref, wb_ref, bb_ref, dvk_ref, end_ref
):
    blocks, _, rows, _ = vk_ref.shape
    width = base_ref.shape[2]
    tiles = width // LANES
    weights = lane_weights(sk, width)
    lane = lane_of(rows)
    low = lane < hd
    causal = lax.broadcasted_iota(jnp.int32, (rows, rows), 0) <= lax.broadcasted_iota(
        jnp.int32, (rows, rows), 1
    )
    state = base_ref[0]
    for c in reversed(range(blocks)):
        after = state.astype(BF16)
        vk = vk_ref[c, 0]
        e0, e1, d0, d1 = sketched(vk, wb_ref[...])
        e, d = e0 * e1, d0 * d1
        qdot = qdot_ref[0, c]
        dn = dn_ref[0, c]
        ones = jnp.where(low, vk.astype(F32), 1.0).astype(BF16)
        dots = jnp.where(causal, mm(kdot_ref[0, c], qdot, NT), 0.0)
        cot_dots = (2.0 * dots * mm(ones, dn, NT)).astype(BF16)
        near = mm(cot_dots, qdot)
        dv = mm(feat_ref[0, c], after, NT) + mm((dots * dots).astype(BF16), dn)
        cot = mm(ones, after)
        cot_e, cot_d = feature_pull(cot, e, d, sk, tiles)
        cot_e = cot_e + jnp.where(lane < 2 * sk, near, 0.0)
        back = jnp.concatenate(
            [(cot_e * e1).astype(BF16), (cot_e * e0).astype(BF16), (cot_d * d1).astype(BF16), (cot_d * d0).astype(BF16)],
            axis=1,
        )
        dvk_ref[c, 0] = (jnp.where(low, dv, 0.0) + mm(back, bb_ref[...])).astype(BF16)
        state = state + cot_ref[0, c] * weights
    end_ref[0] = state


def unpack_query_kernel(hd, dq_ref, w_ref, out_ref, part_ref):
    heads, half, _ = dq_ref.shape
    low = lane_of(half) < hd
    for pair in range(heads // 2):
        a = dq_ref[2 * pair].astype(F32)
        b = dq_ref[2 * pair + 1].astype(F32)
        cols = slice(pair * LANES, (pair + 1) * LANES)
        out_ref[:half, cols] = jnp.where(low, a, pltpu.roll(b, hd, 1)).astype(BF16)
        out_ref[half:, cols] = jnp.where(low, pltpu.roll(a, hd, 1), b).astype(BF16)
    whole = out_ref[...]
    depth = out_ref.shape[1]
    for i in range(w_ref.shape[0] // depth):
        part_ref[i] = mm(whole, w_ref[i * depth : (i + 1) * depth, :], NT)


def unpack_key_kernel(hd, order_ref, dvk_ref, wk_ref, wv_ref, part_ref, dk_ref, dv_ref, out_ref):
    heads, rows, _ = dvk_ref.shape
    low = lane_of(rows) < hd
    for pair in range(heads // 2):
        a = dvk_ref[2 * pair].astype(F32)
        b = dvk_ref[2 * pair + 1].astype(F32)
        cols = slice(pair * LANES, (pair + 1) * LANES)
        dv_ref[:, cols] = jnp.where(low, a, pltpu.roll(b, hd, 1)).astype(BF16)
        dk_ref[:, cols] = jnp.where(low, pltpu.roll(a, hd, 1), b).astype(BF16)
    dk = dk_ref[...]
    dv = dv_ref[...]
    depth = dk_ref.shape[1]
    for i in range(out_ref.shape[0]):
        block = order_ref[i]
        at = pl.ds(pl.multiple_of(block * depth, depth), depth)
        total = part_ref[block] + mm(dk, wk_ref[at, :], NT) + mm(dv, wv_ref[at, :], NT)
        out_ref[i] = total.astype(BF16)


def expand_kernel(hd, all_ref, dstate_ref, dnorm_ref, map_ref, state_ref, norm_ref):
    heads, rows, width = all_ref.shape
    flat = all_ref[...].reshape(heads * rows, width)
    spread = mm(flat, map_ref[...], NT)
    for h in range(heads):
        state_ref[h] = dstate_ref[h] + spread[h * rows : h * rows + hd]
        norm_ref[h : h + 1] = dnorm_ref[h : h + 1] + spread[h * rows + hd : h * rows + hd + 1] * float(LANES - hd)


def params(mib, **more):
    return pltpu.CompilerParams(vmem_limit_bytes=mib * MIB, **more)


def shape(dims, kind):
    return jax.ShapeDtypeStruct(dims, kind)


def spec(block, index=None):
    if index is None:
        index = lambda h, *_: (h,) + (0,) * (len(block) - 1)
    return pl.BlockSpec(block, index)


def fixed(array):
    dims = array.shape
    return pl.BlockSpec(dims, lambda *_: (0,) * len(dims))


def hop(x, axis, distance):
    count = lax.axis_size(axis)
    return lax.ppermute(x, axis, [(i, i ^ distance) for i in range(count)])


def body(groups, local, inputs, w_query, w_key, w_value, sketch, prefix_state, prefix_norm, d_attn, d_state_end, d_norm_end):
    rows, depth = inputs.shape
    width = w_query.shape[1]
    heads, feat, hd = prefix_state.shape
    sk = sketch.shape[2]
    tiles = tile_count(sk)
    lanes = tiles * LANES
    half = rows // 2
    mine = heads // local
    ranks = lax.axis_size("head")
    rank = lax.axis_index("head")
    place = lax.axis_index("local")
    group = lax.axis_index("group")

    def exchange(x):
        return lax.all_to_all(x, "local", 0, 0, tiled=True) if local > 1 else x

    pieces = {0: inputs}
    distance = ranks // 2
    while distance:
        pieces.update({at ^ distance: hop(x, "head", distance) for at, x in list(pieces.items())})
        distance //= 2
    keys = sorted(pieces)
    where = jnp.stack([rank ^ at for at in keys]).astype(jnp.int32)

    grad = d_attn.reshape(2, half, heads, hd).transpose(2, 1, 0, 3).reshape(heads, half, 2 * hd)
    grad = exchange(grad).reshape(local, mine, half, LANES)

    step = LANES // sk
    left, right = sketch[0], sketch[1] * sk ** (-0.5)
    turns = np.concatenate([(np.arange(sk) + j) % sk for j in range(step)])
    full = jnp.concatenate(
        [jnp.tile(left, (1, step)), jnp.tile(right, (1, step)), left[:, turns], right[:, turns]], axis=1
    )
    hi = lax.reduce_precision(full, 8, 7)
    lo = (full - hi).astype(BF16)
    hi = hi.astype(BF16)
    none = jnp.zeros_like(hi)
    wa = jnp.concatenate([hi, none, lo, none], axis=0)
    wb = jnp.concatenate([none, hi, none, lo], axis=0)
    ba = jnp.concatenate([hi, none], axis=0).T
    bb = jnp.concatenate([none, hi], axis=0).T
    table = jnp.asarray(pair_map(sk), BF16)

    state_t = prefix_state.transpose(0, 2, 1)
    dstate_t = d_state_end.transpose(0, 2, 1)
    start = (place * mine).astype(jnp.int32)[None]
    one_head = pl.BlockSpec((1, hd, feat), lambda h, s: (s[0] + h, 0, 0))
    state_spec = spec((1, LANES, lanes))
    base, base_after = pl.pallas_call(
        partial(base_kernel, sk),
        grid_spec=pltpu.PrefetchScalarGridSpec(
            num_scalar_prefetch=1,
            grid=(mine,),
            in_specs=[one_head, fixed(prefix_norm), one_head, fixed(d_norm_end), fixed(table)],
            out_specs=[state_spec] * 2,
            scratch_shapes=[pltpu.VMEM((2, heads, lanes), F32)],
        ),
        out_shape=[shape((mine, LANES, lanes), F32)] * 2,
        compiler_params=params(24),
        name="base_states",
    )(start, state_t, prefix_norm, dstate_t, d_norm_end, table)

    smem = pl.BlockSpec(memory_space=pltpu.SMEM)
    vmem = pl.BlockSpec(memory_space=pltpu.VMEM)

    def project(name, weights, out_rows):
        return pl.pallas_call(
            partial(project_kernel, hd, len(keys)),
            in_specs=[smem] + [vmem] * (len(keys) + len(weights)),
            out_specs=vmem,
            out_shape=shape((heads, out_rows, LANES), BF16),
            compiler_params=params(24),
            name=name,
        )(where, *[pieces[at] for at in keys], *weights)

    vk = project("project_key_value", (w_value, w_key), rows)
    vk = exchange(vk).reshape(local, mine, rows, LANES)
    query = project("project_query", (w_query,), half)
    query = exchange(query).reshape(local, mine, half, LANES)

    across = lambda n: spec((local, 1, n, LANES), lambda h: (0, h, 0, 0))
    own = lambda *dims: spec((1,) + dims, lambda h: (h,) + (0,) * len(dims))

    def key_side(start_state):
        return pl.pallas_call(
            partial(key_kernel, sk, hd),
            grid=(mine,),
            in_specs=[across(rows), state_spec, fixed(wb)],
            out_specs=[own(local, LANES, lanes), own(local, rows, lanes), own(local, rows, LANES), state_spec],
            out_shape=[
                shape((mine, local, LANES, lanes), BF16),
                shape((mine, local, rows, lanes), BF16),
                shape((mine, local, rows, LANES), BF16),
                shape((mine, LANES, lanes), F32),
            ],
            compiler_params=params(32),
            name="key_side",
        )(vk, start_state, wb)

    def of_groups(x, wanted):
        everything = lax.all_gather(x.astype(BF16), "group").astype(F32)
        chosen = wanted(jnp.arange(groups))
        return jnp.where(chosen.reshape((groups,) + (1,) * x.ndim), everything, 0.0).sum(0)

    if groups > 1:
        sums = key_side(jnp.zeros_like(base))[3]
        base = base + of_groups(sums, lambda at: at < group)
    states, key_feats, kdot, _ = key_side(base)

    query_out = pl.pallas_call(
        partial(query_kernel, sk, hd),
        grid=(mine,),
        in_specs=[
            across(half), across(half), across(rows), own(local, rows, LANES), own(local, LANES, lanes),
            fixed(wa), fixed(wb), fixed(ba), fixed(bb),
        ],
        out_specs=[
            across(half), own(local, rows, LANES), own(local, rows, LANES), own(local, LANES, lanes),
            own(hd + 16, lanes),
        ],
        out_shape=[
            shape((local, mine, half, LANES), BF16),
            shape((mine, local, rows, LANES), BF16),
            shape((mine, local, rows, LANES), BF16),
            shape((mine, local, LANES, lanes), F32),
            shape((mine, hd + 16, lanes), BF16),
        ],
        compiler_params=params(48),
        name="query_side",
    )(query, grad, vk, kdot, states, wa, wb, ba, bb)
    dq, qdot, dn, cots, window = query_out
    dq = exchange(dq.reshape(heads, half, LANES))

    if groups > 1:
        scale = np.where(np.arange(lanes) >= 0, 1.0, 0.0).astype(np.float32)
        later = of_groups(cots.sum(1), lambda at: at > group)
        base_after = base_after + later * lane_weights(sk, lanes)

    dvk, _ = pl.pallas_call(
        partial(reverse_kernel, sk, hd),
        grid=(mine,),
        in_specs=[
            across(rows), own(local, rows, lanes), own(local, rows, LANES), own(local, rows, LANES),
            own(local, rows, LANES), own(local, LANES, lanes), state_spec, fixed(wb), fixed(bb),
        ],
        out_specs=[across(rows), state_spec],
        out_shape=[shape((local, mine, rows, LANES), BF16), shape((mine, LANES, lanes), F32)],
        compiler_params=params(48),
        name="key_gradients",
    )(vk, key_feats, kdot, qdot, dn, cots, base_after, wb, bb)
    dvk = exchange(dvk.reshape(heads, rows, LANES))

    if groups > 1:
        window = lax.psum(window, "group")
    window = lax.all_gather(window, "local", axis=0, tiled=True)
    state_out, d_prefix_norm = pl.pallas_call(
        partial(expand_kernel, hd),
        in_specs=[vmem] * 4,
        out_specs=[vmem] * 2,
        out_shape=[shape((heads, hd, feat), F32), shape((heads, feat), F32)],
        compiler_params=params(32),
        name="prefix_gradients",
    )(window, dstate_t, d_norm_end, table)
    d_prefix_state = state_out.transpose(0, 2, 1)

    d_query, part = pl.pallas_call(
        partial(unpack_query_kernel, hd),
        in_specs=[vmem] * 2,
        out_specs=[vmem] * 2,
        out_shape=[shape((rows, width), BF16), shape((ranks, rows, depth), F32)],
        compiler_params=params(24),
        name="input_from_query",
    )(dq, w_query)

    order, distance = [0], 1
    while distance < ranks:
        order = [at for at in range(ranks)]
        distance *= 2
    order = sorted(range(ranks), key=lambda at: [-(at >> bit & 1) for bit in range(ranks.bit_length() - 1)])
    order_of = jnp.stack([rank ^ at for at in order]).astype(jnp.int32)
    d_key, d_value, sums = pl.pallas_call(
        partial(unpack_key_kernel, hd),
        in_specs=[smem] + [vmem] * 4,
        out_specs=[vmem] * 3,
        out_shape=[shape((rows, width), BF16), shape((rows, width), BF16), shape((ranks, rows, depth), BF16)],
        compiler_params=params(32),
        name="input_from_key_value",
    )(order_of, dvk, w_key, w_value, part)
    distance = 1
    while distance < ranks:
        count = sums.shape[0] // 2
        came = hop(sums[:count], "head", distance)
        sums = (sums[count:].astype(F32) + came.astype(F32)).astype(BF16)
        distance *= 2
    return sums[0], d_query, d_key, d_value, d_prefix_state, d_prefix_norm


def solution(mesh):
    seq, head = mesh.shape["seq"], mesh.shape["head"]

    def run(*args):
        heads = args[5].shape[0] // head
        local = math.gcd(heads, seq)
        groups = seq // local
        inner = Mesh(mesh.devices.reshape(groups, local, head), ("group", "local", "head"))
        tokens = ("group", "local")
        return jax.shard_map(
            partial(body, groups, local),
            mesh=inner,
            in_specs=(
                P(tokens, "head"),
                P(None, "head"),
                P(None, "head"),
                P(None, "head"),
                P(),
                P("head", None, None),
                P("head", None),
                P(tokens, "head"),
                P("head", None, None),
                P("head", None),
            ),
            out_specs=(
                P(tokens, "head"),
                P(tokens, "head"),
                P(tokens, "head"),
                P(tokens, "head"),
                P("head", None, None),
                P("head", None),
            ),
            check_vma=False,
        )(*args)

    return run
```

```python
import math
from functools import partial

import jax
import jax.numpy as jnp
import numpy as np
from jax import lax
from jax.experimental import pallas as pl
from jax.experimental.pallas import tpu as pltpu
from jax.sharding import Mesh, PartitionSpec as P

F32 = jnp.float32
BF16 = jnp.bfloat16
LANES = 128
VMEM = pltpu.VMEM
MIB = 1024 * 1024

NN = (((1,), (0,)), ((), ()))
NT = (((1,), (1,)), ((), ()))
TN = (((0,), (0,)), ((), ()))


def mm(a, b, dims=NN):
    return lax.dot_general(a, b, dims, preferred_element_type=F32)


def split(x):
    hi = x.astype(BF16)
    return hi, (x - hi.astype(F32)).astype(BF16)


def tile_count(sk):
    return -(-(sk // 2 + 1) // (LANES // sk))


def pair_map(sk):
    step = LANES // sk
    width = tile_count(sk) * LANES
    lane = np.arange(width)
    tile, within = lane // LANES, lane % LANES
    j, a = within // sk, within % sk
    first, second = (a + j) % sk, (a - step * tile) % sk
    keep = step * tile + j <= sk // 2
    table = np.zeros((sk * sk, width), np.float32)
    for one in lane[keep]:
        x, y = first[one], second[one]
        r = step * tile[one] + j[one]
        if r == 0:
            table[x * sk + y, one] = 1.0
        else:
            value = 0.5 if 2 * r == sk else 1.0
            table[x * sk + y, one] = value
            table[y * sk + x, one] = value
    return table


def lane_weights(sk, width):
    lane = lax.broadcasted_iota(jnp.int32, (1, width), 1)
    r = (LANES // sk) * (lane // LANES) + (lane % LANES) // sk
    return jnp.where(
        r <= sk // 2, jnp.where((r == 0) | (2 * r == sk), 1.0, 2.0), 0.0
    ).astype(F32)


def sketched(x, weights):
    both = mm(jnp.concatenate([x, x], axis=1), weights)
    return tuple(both[:, LANES * i : LANES * (i + 1)] for i in range(4))


def turned(e, sk, tiles):
    step = LANES // sk
    return [e] + [pltpu.roll(e, step * t, 1) for t in range(1, tiles)]


def features(e, d, sk, tiles):
    return jnp.concatenate([(d * x).astype(BF16) for x in turned(e, sk, tiles)], axis=1)


def feature_pull(cot, e, d, sk, tiles):
    step = LANES // sk
    cot_e = cot_d = None
    for t, x in enumerate(turned(e, sk, tiles)):
        part = cot[:, LANES * t : LANES * (t + 1)]
        to_d = part * x
        to_e = part * d
        if t:
            to_e = pltpu.roll(to_e, LANES - step * t, 1)
        cot_d = to_d if cot_d is None else cot_d + to_d
        cot_e = to_e if cot_e is None else cot_e + to_e
    return cot_e, cot_d


def lane_of(rows):
    return lax.broadcasted_iota(jnp.int32, (rows, LANES), 1)


def slot_of(place, other, local):
    return lax.rem(other - place + local, local)


def came_in(place, other, local):
    return lax.rem(place - other + local, local)


def prepare_kernel(
    sk, place_ref, sketch_ref, state_ref, norm_ref, dstate_ref, dnorm_ref, map_ref,
    fwd_ref, bwd_ref, wa_ref, wb_ref, ba_ref, bb_ref, rows_ref,
):
    table = map_ref[...]
    mine, half, _ = state_ref.shape
    step = LANES // sk
    left, right = sketch_ref[0], sketch_ref[1] * sk ** (-0.5)

    def turns(x):
        return [x] + [jnp.concatenate([x[j:], x[:j]], axis=0) for j in range(1, step)]

    full = jnp.concatenate([left] * step + [right] * step + turns(left) + turns(right), axis=0)
    hi, lo = split(full)
    none = jnp.zeros_like(full)
    ba_ref[...] = jnp.concatenate([hi.astype(F32), none], axis=1).astype(BF16)
    bb_ref[...] = jnp.concatenate([none, hi.astype(F32)], axis=1).astype(BF16)
    hi, lo = hi.astype(F32).T, lo.astype(F32).T
    none = jnp.zeros_like(hi)
    wa_ref[...] = jnp.concatenate([hi, none, lo, none], axis=0).astype(BF16)
    wb_ref[...] = jnp.concatenate([none, hi, none, lo], axis=0).astype(BF16)

    def mapped(x):
        hi, lo = split(x)
        return mm(hi, table) + mm(lo, table)

    for which, (s_ref, n_ref, o_ref, scale) in enumerate(
        ((state_ref, norm_ref, fwd_ref, 1.0), (dstate_ref, dnorm_ref, bwd_ref, 1.0 / half))
    ):
        rows_ref[which] = mapped(n_ref[...]) * scale
        for m in range(mine):
            o_ref[m, :half] = mapped(s_ref[m])
            o_ref[m, half:] = jnp.broadcast_to(
                rows_ref[which, pl.ds(place_ref[0] * mine + m, 1), :], (LANES - half, o_ref.shape[2])
            )


def gradient_kernel(hd, local, grad_ref, out_ref):
    rows = grad_ref.shape[0]
    half = rows // 2
    low = lane_of(half) < hd
    mine = out_ref.shape[1]
    for pair in range(local * mine // 2):
        both = grad_ref[:, pair * LANES : (pair + 1) * LANES].astype(F32)
        top, bottom = both[:half], both[half:]
        for at, block in (
            (2 * pair, jnp.where(low, top, pltpu.roll(bottom, hd, 1))),
            (2 * pair + 1, jnp.where(low, pltpu.roll(top, hd, 1), bottom)),
        ):
            out_ref[at // mine, at % mine] = block.astype(BF16)


def bring(weights, where_ref, depth, held_ref, done_ref):
    copies = [
        [
            pltpu.make_async_copy(
                w.at[pl.ds(pl.multiple_of(where_ref[i] * depth, depth), depth)], held_ref.at[k, i], done_ref.at[k, i]
            )
            for i in range(held_ref.shape[1])
        ]
        for k, w in enumerate(weights)
    ]
    for i in range(held_ref.shape[1]):
        for k in range(len(weights)):
            copies[k][i].start()
    return copies


def project_kernel(hd, local, count, place_ref, where_ref, *refs):
    pieces = refs[:count]
    weights = refs[count : count + 3]
    out_refs = refs[count + 3 : -3]
    blocks_ref, held_ref, done_ref = refs[-3:]
    depth = pieces[0].shape[1]
    rows = pieces[0].shape[0]
    half = rows // 2
    mine = blocks_ref.shape[1]
    copies = bring(weights, where_ref, depth, held_ref, done_ref)
    sums = []
    for k in range(len(weights)):
        total = None
        for i, x in enumerate(pieces):
            copies[k][i].wait()
            part = mm(x[...], held_ref[k, i])
            total = part if total is None else total + part
        sums.append(total)
    value, key, query = sums
    for h in range(local * mine):
        cols = slice(h * hd, (h + 1) * hd)
        slot = slot_of(place_ref[0], h // mine, local)
        blocks_ref[slot, h % mine, :rows] = jnp.concatenate([value[:, cols], key[:, cols]], axis=1).astype(BF16)
        blocks_ref[slot, h % mine, rows:] = jnp.concatenate(
            [query[:half, cols], query[half:, cols]], axis=1
        ).astype(BF16)
    for s, out_ref in enumerate(out_refs):
        out_ref[...] = blocks_ref[s]


def key_kernel(sk, hd, local, place_ref, *refs):
    slots = refs[:local]
    base_ref, wb_ref, qkv_ref, state_ref, feat_ref, kdot_ref, total_ref = refs[local:]
    blocks, mine, packed, _ = qkv_ref.shape
    for s, slot in enumerate(slots):
        qkv_ref[came_in(place_ref[0], s, blocks)] = slot[...]
    rows = packed * 2 // 3
    width = base_ref.shape[2]
    tiles = width // LANES
    weights = lane_weights(sk, width)
    lane = lane_of(rows)
    for m in range(mine):
        state = base_ref[m]
        for c in range(blocks):
            state_ref[m, c] = state.astype(BF16)
            vk = qkv_ref[c, m, :rows]
            e0, e1, d0, d1 = sketched(vk, wb_ref[...])
            e, d = e0 * e1, d0 * d1
            feat = features(e, d, sk, tiles)
            feat_ref[m, c] = feat
            hi, lo = split(e)
            kdot_ref[m, c] = jnp.where(
                lane < 2 * sk, hi.astype(F32), jnp.where(lane < 3 * sk, lo.astype(F32), 0.0)
            ).astype(BF16)
            ones = jnp.where(lane < hd, vk.astype(F32), 1.0).astype(BF16)
            state = state + mm(ones, feat, TN) * weights
        total_ref[m] = state


def query_kernel(
    sk, hd, qkv_ref, g_ref, kdot_ref, state_ref, wa_ref, wb_ref, ba_ref, bb_ref,
    dq_ref, qdot_ref, dn_ref, cot_ref, total_ref,
):
    blocks, mine, packed, _ = qkv_ref.shape
    rows = packed * 2 // 3
    half = rows // 2
    width = state_ref.shape[3]
    tiles = width // LANES
    lane = lane_of(rows)
    low = lane < hd
    causal = lax.broadcasted_iota(jnp.int32, (rows, rows), 0) >= lax.broadcasted_iota(
        jnp.int32, (rows, rows), 1
    )
    r_i = lax.broadcasted_iota(jnp.int32, (2 * LANES, LANES), 0) % LANES
    c_i = lax.broadcasted_iota(jnp.int32, (2 * LANES, LANES), 1)
    adder = jnp.where((r_i < hd) & (c_i >= hd), -1.0 / (LANES - hd), 0.0).astype(BF16)
    for m in range(mine):
        total = jnp.zeros((LANES, width), F32)
        for c in range(blocks):
            q = qkv_ref[c, m, rows:]
            top = sketched(q, wa_ref[...])
            bottom = sketched(q, wb_ref[...])
            e0, e1, d0, d1 = tuple(jnp.concatenate([a, b], axis=0) for a, b in zip(top, bottom))
            e, d = e0 * e1, d0 * d1
            feat = features(e, d, sk, tiles)
            hi, lo = split(e)
            qdot = jnp.where(
                (lane >= sk) & (lane < 2 * sk),
                lo.astype(F32),
                jnp.where(lane < 3 * sk, hi.astype(F32), 0.0),
            ).astype(BF16)
            qdot_ref[m, c] = qdot
            kdot = kdot_ref[m, c]
            state = state_ref[m, c]
            ones = jnp.where(low, qkv_ref[c, m, :rows].astype(F32), 1.0).astype(BF16)
            dots = jnp.where(causal, mm(qdot, kdot, NT), 0.0)
            num = mm(feat, state, NT) + mm((dots * dots).astype(BF16), ones)
            inv = 1.0 / (1.0 + num)
            inv = jnp.where(low, pltpu.roll(inv, hd, 1), inv)
            g = g_ref[c, m].astype(F32)
            g = jnp.concatenate([g, pltpu.roll(g, hd, 1)], axis=0)
            g_hi, g_lo = split(jnp.where(low, g * num, 0.0))
            den = mm(jnp.concatenate([g_hi, g_lo], axis=1), adder)
            dn = (jnp.where(low, g, den * inv) * inv).astype(BF16)
            dn_ref[m, c] = dn
            cot_dots = (2.0 * dots * mm(dn, ones, NT)).astype(BF16)
            near = mm(cot_dots, kdot)
            cot = mm(dn, state)
            cot_e, cot_d = feature_pull(cot, e, d, sk, tiles)
            cot_e = cot_e + jnp.where((lane < sk) | (lane >= 2 * sk), near, 0.0)
            back = jnp.concatenate(
                [
                    (cot_e * e1).astype(BF16),
                    (cot_e * e0).astype(BF16),
                    (cot_d * d1).astype(BF16),
                    (cot_d * d0).astype(BF16),
                ],
                axis=1,
            )
            dq_ref[m, c] = (mm(back[:half], ba_ref[...]) + mm(back[half:], bb_ref[...])).astype(BF16)
            here = mm(dn, feat, TN)
            cot_ref[m, c] = here
            total = total + here
        total_ref[m] = total[: total_ref.shape[1]].astype(BF16)


def reverse_kernel(
    sk, hd, place_ref, qkv_ref, dq_ref, feat_ref, kdot_ref, qdot_ref, dn_ref, cot_ref, base_ref, wb_ref, bb_ref, *refs
):
    out_refs = refs[:-1]
    blocks_ref = refs[-1]
    blocks, mine, packed, _ = qkv_ref.shape
    rows = packed * 2 // 3
    width = base_ref.shape[2]
    tiles = width // LANES
    weights = lane_weights(sk, width)
    lane = lane_of(rows)
    low = lane < hd
    causal = lax.broadcasted_iota(jnp.int32, (rows, rows), 0) <= lax.broadcasted_iota(
        jnp.int32, (rows, rows), 1
    )
    for m in range(mine):
        state = base_ref[m]
        for c in reversed(range(blocks)):
            after = state.astype(BF16)
            vk = qkv_ref[c, m, :rows]
            e0, e1, d0, d1 = sketched(vk, wb_ref[...])
            e, d = e0 * e1, d0 * d1
            qdot = qdot_ref[m, c]
            dn = dn_ref[m, c]
            ones = jnp.where(low, vk.astype(F32), 1.0).astype(BF16)
            dots = jnp.where(causal, mm(kdot_ref[m, c], qdot, NT), 0.0)
            cot_dots = (2.0 * dots * mm(ones, dn, NT)).astype(BF16)
            near = mm(cot_dots, qdot)
            dv = mm(feat_ref[m, c], after, NT) + mm((dots * dots).astype(BF16), dn)
            cot = mm(ones, after)
            cot_e, cot_d = feature_pull(cot, e, d, sk, tiles)
            cot_e = cot_e + jnp.where(lane < 2 * sk, near, 0.0)
            back = jnp.concatenate(
                [
                    (cot_e * e1).astype(BF16),
                    (cot_e * e0).astype(BF16),
                    (cot_d * d1).astype(BF16),
                    (cot_d * d0).astype(BF16),
                ],
                axis=1,
            )
            slot = slot_of(place_ref[0], c, blocks)
            blocks_ref[slot, m, :rows] = (jnp.where(low, dv, 0.0) + mm(back, bb_ref[...])).astype(BF16)
            blocks_ref[slot, m, rows:] = dq_ref[m, c]
            state = state + cot_ref[m, c] * weights
    for s, out_ref in enumerate(out_refs):
        out_ref[...] = blocks_ref[s]


def input_kernel(hd, local, place_ref, order_ref, *refs):
    slots = refs[:local]
    weights = refs[local : local + 3]
    dq_ref, dk_ref, dv_ref, out_ref, all_ref, held_ref, done_ref = refs[local + 3 :]
    copies = bring(weights, order_ref, dk_ref.shape[1], held_ref, done_ref)
    _, mine, packed, _ = all_ref.shape
    for s, slot in enumerate(slots):
        all_ref[came_in(place_ref[0], s, local)] = slot[...]
    rows = packed * 2 // 3
    half = rows // 2
    low = lane_of(rows) < hd

    def block(head):
        return all_ref[head // mine, head % mine].astype(F32)

    for pair in range(local * mine // 2):
        a, b = block(2 * pair), block(2 * pair + 1)
        cols = slice(pair * LANES, (pair + 1) * LANES)
        dv_ref[:, cols] = jnp.where(low, a[:rows], pltpu.roll(b[:rows], hd, 1)).astype(BF16)
        dk_ref[:, cols] = jnp.where(low, pltpu.roll(a[:rows], hd, 1), b[:rows]).astype(BF16)
        a, b = a[rows:], b[rows:]
        dq_ref[:half, cols] = jnp.where(low[:half], a, pltpu.roll(b, hd, 1)).astype(BF16)
        dq_ref[half:, cols] = jnp.where(low[:half], pltpu.roll(a, hd, 1), b).astype(BF16)
    dq, dk, dv = dq_ref[...], dk_ref[...], dv_ref[...]
    for i in range(out_ref.shape[0]):
        total = None
        for k, x in enumerate((dq, dk, dv)):
            copies[k][i].wait()
            part = mm(x, held_ref[k, i], NT)
            total = part if total is None else total + part
        out_ref[i] = total.astype(BF16)


def expand_kernel(hd, local, place_ref, *refs):
    pieces = refs[:local]
    dstate_ref, dnorm_ref, map_ref, state_ref, norm_ref, all_ref = refs[local:]
    mine, rows, width = pieces[0].shape
    for k, piece in enumerate(pieces):
        all_ref[lax.bitwise_xor(place_ref[0], k)] = piece[...]
    heads = local * mine
    spread = mm(all_ref[...].reshape(heads * rows, width), map_ref[...], NT)
    for h in range(heads):
        state_ref[h] = dstate_ref[h] + spread[h * rows : h * rows + hd]
        norm_ref[h : h + 1] = dnorm_ref[h : h + 1] + spread[h * rows + hd : h * rows + hd + 1] * float(LANES - hd)


def call(kernel, name, out_shape, scalars, arrays, stay=(), mib=16, scratch=()):
    smem = pl.BlockSpec(memory_space=pltpu.SMEM)
    vmem = pl.BlockSpec(memory_space=pltpu.VMEM)
    return pl.pallas_call(
        kernel,
        in_specs=[smem] * len(scalars) + [vmem] * len(arrays) + [pl.BlockSpec(memory_space=pl.ANY)] * len(stay),
        out_specs=[vmem] * len(out_shape),
        out_shape=[jax.ShapeDtypeStruct(dims, kind) for dims, kind in out_shape],
        scratch_shapes=list(scratch),
        compiler_params=pltpu.CompilerParams(vmem_limit_bytes=mib * MIB),
        name=name,
    )(*scalars, *arrays, *stay)


def hop(x, axis, distance):
    count = lax.axis_size(axis)
    return lax.ppermute(x, axis, [(i, i ^ distance) for i in range(count)])


def body(groups, local, inputs, w_query, w_key, w_value, sketch, prefix_state, prefix_norm, d_attn, d_state_end, d_norm_end):
    rows, depth = inputs.shape
    width = w_query.shape[1]
    heads, feat, hd = prefix_state.shape
    sk = sketch.shape[2]
    tiles = tile_count(sk)
    lanes = tiles * LANES
    half = rows // 2
    packed = rows + half
    mine = heads // local
    ranks = lax.axis_size("head")
    rank = lax.axis_index("head")
    place = lax.axis_index("local")
    group = lax.axis_index("group")
    here = place.astype(jnp.int32)[None]

    def send(x, shift):
        return lax.ppermute(x, "local", [(i, (i + shift) % local) for i in range(local)])

    def exchange(x):
        order = sorted(range(1, local), key=lambda s: -min(s, local - s))
        came = {s: send(x[s], s) for s in order}
        came[0] = x[0]
        return [came[s] for s in range(local)]

    pieces = {0: inputs}
    distance = ranks // 2
    while distance:
        pieces.update({at ^ distance: hop(x, "head", distance) for at, x in list(pieces.items())})
        distance //= 2
    keys = sorted(pieces)
    where = jnp.stack([rank ^ at for at in keys]).astype(jnp.int32)

    (grad,) = call(
        partial(gradient_kernel, hd, local), "gather_cotangents", [((local, mine, half, LANES), BF16)], [], [d_attn]
    )
    grad = lax.all_to_all(grad, "local", 0, 0, tiled=True)

    table = jnp.asarray(pair_map(sk), BF16)

    state_t = prefix_state.transpose(0, 2, 1)
    dstate_t = d_state_end.transpose(0, 2, 1)
    own = lambda x: lax.dynamic_slice_in_dim(x, place * mine, mine, 0)
    base, base_after, wa, wb, ba, bb = call(
        partial(prepare_kernel, sk),
        "prepare",
        [((mine, LANES, lanes), F32)] * 2 + [((4 * hd, 4 * LANES), BF16)] * 2 + [((4 * LANES, 2 * hd), BF16)] * 2,
        [here],
        [sketch.transpose(0, 2, 1), own(state_t), prefix_norm, own(dstate_t), d_norm_end, table],
        scratch=[pltpu.VMEM((2, heads, lanes), F32)],
    )
    early = lax.optimization_barrier((pieces[keys[-1]], grad, base, base_after, wa, wb, ba, bb))
    pieces[keys[-1]], grad, base, base_after, wa, wb, ba, bb = early

    block = ((mine, packed, LANES), BF16)
    all_blocks = pltpu.VMEM((local,) + block[0], BF16)
    held = [pltpu.VMEM((3, ranks, depth, width), BF16), pltpu.SemaphoreType.DMA((3, ranks))]
    slots = call(
        partial(project_kernel, hd, local, len(keys)),
        "project",
        [block] * local,
        [here, where],
        [pieces[at] for at in keys],
        [w_value, w_key, w_query],
        scratch=[all_blocks] + held,
    )
    slots = exchange(slots)

    def key_side(start_state):
        return call(
            partial(key_kernel, sk, hd, local),
            "key_side",
            [
                ((local, mine, packed, LANES), BF16),
                ((mine, local, LANES, lanes), BF16),
                ((mine, local, rows, lanes), BF16),
                ((mine, local, rows, LANES), BF16),
                ((mine, LANES, lanes), F32),
            ],
            [here],
            [*slots, start_state, wb],
        )

    def of_groups(x, wanted):
        everything = lax.all_gather(x.astype(BF16), "group").astype(F32)
        chosen = wanted(jnp.arange(groups))
        return jnp.where(chosen.reshape((groups,) + (1,) * x.ndim), everything, 0.0).sum(0)

    if groups > 1:
        sums = key_side(jnp.zeros_like(base))[4]
        base = base + of_groups(sums, lambda at: at < group)
    qkv, states, key_feats, kdot, _ = key_side(base)

    dq, qdot, dn, cots, window = call(
        partial(query_kernel, sk, hd),
        "query_side",
        [
            ((mine, local, half, LANES), BF16),
            ((mine, local, rows, LANES), BF16),
            ((mine, local, rows, LANES), BF16),
            ((mine, local, LANES, lanes), F32),
            ((mine, hd + 16, lanes), BF16),
        ],
        [],
        [qkv, grad, kdot, states, wa, wb, ba, bb],
    )
    if groups > 1:
        later = of_groups(cots.sum(1), lambda at: at > group)
        base_after = base_after + later * lane_weights(sk, lanes)

    gradients = call(
        partial(reverse_kernel, sk, hd),
        "key_gradients",
        [block] * local,
        [here],
        [qkv, dq, key_feats, kdot, qdot, dn, cots, base_after, wb, bb],
        scratch=[all_blocks],
    )
    gradients = exchange(gradients)

    if groups > 1:
        window = lax.psum(window, "group")
    spread = {0: window}
    distance = local // 2
    while distance:
        both = jnp.stack([spread[at] for at in sorted(spread)])
        both = hop(both, "local", distance)
        spread.update({at ^ distance: both[n] for n, at in enumerate(sorted(spread))})
        distance //= 2

    order = sorted(range(ranks), key=lambda at: [-(at >> bit & 1) for bit in range(ranks.bit_length() - 1)])
    order_of = jnp.stack([rank ^ at for at in order]).astype(jnp.int32)
    d_query, d_key, d_value, sums = call(
        partial(input_kernel, hd, local),
        "input_gradient",
        [((rows, width), BF16)] * 3 + [((ranks, rows, depth), BF16)],
        [here, order_of],
        gradients,
        [w_query, w_key, w_value],
        scratch=[all_blocks] + held,
    )
    distance = 1
    while distance < ranks:
        count = sums.shape[0] // 2
        came = hop(sums[:count], "head", distance)
        sums = (sums[count:].astype(F32) + came.astype(F32)).astype(BF16)
        distance *= 2

    state_out, d_prefix_norm = call(
        partial(expand_kernel, hd, local),
        "prefix_gradients",
        [((heads, hd, feat), F32), ((heads, feat), F32)],
        [here],
        [*[spread[k] for k in range(local)], dstate_t, d_norm_end, table],
        scratch=[pltpu.VMEM((local,) + window.shape, BF16)],
    )
    d_prefix_state = state_out.transpose(0, 2, 1)
    return sums[0], d_query, d_key, d_value, d_prefix_state, d_prefix_norm


def solution(mesh):
    seq, head = mesh.shape["seq"], mesh.shape["head"]

    def run(*args):
        heads = args[5].shape[0] // head
        local = math.gcd(heads, seq)
        groups = seq // local
        inner = Mesh(mesh.devices.reshape(groups, local, head), ("group", "local", "head"))
        tokens = ("group", "local")
        return jax.shard_map(
            partial(body, groups, local),
            mesh=inner,
            in_specs=(
                P(tokens, "head"),
                P(None, "head"),
                P(None, "head"),
                P(None, "head"),
                P(),
                P("head", None, None),
                P("head", None),
                P(tokens, "head"),
                P("head", None, None),
                P("head", None),
            ),
            out_specs=(
                P(tokens, "head"),
                P(tokens, "head"),
                P(tokens, "head"),
                P(tokens, "head"),
                P("head", None, None),
                P("head", None),
            ),
            check_vma=False,
        )(*args)

    return run
```

```python
import math
from functools import partial

import jax
import jax.numpy as jnp
import numpy as np
from jax import lax
from jax.experimental import pallas as pl
from jax.experimental.pallas import tpu as pltpu
from jax.sharding import Mesh, PartitionSpec as P

F32 = jnp.float32
BF16 = jnp.bfloat16
LANES = 128
VMEM = pltpu.VMEM
MIB = 1024 * 1024

NN = (((1,), (0,)), ((), ()))
NT = (((1,), (1,)), ((), ()))
TN = (((0,), (0,)), ((), ()))


def mm(a, b, dims=NN):
    return lax.dot_general(a, b, dims, preferred_element_type=F32)


def split(x):
    hi = x.astype(BF16)
    return hi, (x - hi.astype(F32)).astype(BF16)


def tile_count(sk):
    return -(-(sk // 2 + 1) // (LANES // sk))


def pair_map(sk):
    step = LANES // sk
    width = tile_count(sk) * LANES
    lane = np.arange(width)
    tile, within = lane // LANES, lane % LANES
    j, a = within // sk, within % sk
    first, second = (a + j) % sk, (a - step * tile) % sk
    keep = step * tile + j <= sk // 2
    table = np.zeros((sk * sk, width), np.float32)
    for one in lane[keep]:
        x, y = first[one], second[one]
        r = step * tile[one] + j[one]
        if r == 0:
            table[x * sk + y, one] = 1.0
        else:
            value = 0.5 if 2 * r == sk else 1.0
            table[x * sk + y, one] = value
            table[y * sk + x, one] = value
    return table


def lane_weights(sk, width):
    lane = lax.broadcasted_iota(jnp.int32, (1, width), 1)
    r = (LANES // sk) * (lane // LANES) + (lane % LANES) // sk
    return jnp.where(
        r <= sk // 2, jnp.where((r == 0) | (2 * r == sk), 1.0, 2.0), 0.0
    ).astype(F32)


def sketched(x, weights):
    both = mm(jnp.concatenate([x, x], axis=1), weights)
    return tuple(both[:, LANES * i : LANES * (i + 1)] for i in range(4))


def turned(e, sk, tiles):
    step = LANES // sk
    return [e] + [pltpu.roll(e, step * t, 1) for t in range(1, tiles)]


def features(e, d, sk, tiles):
    return jnp.concatenate([(d * x).astype(BF16) for x in turned(e, sk, tiles)], axis=1)


def feature_pull(cot, e, d, sk, tiles):
    step = LANES // sk
    cot_e = cot_d = None
    for t, x in enumerate(turned(e, sk, tiles)):
        part = cot[:, LANES * t : LANES * (t + 1)]
        to_d = part * x
        to_e = part * d
        if t:
            to_e = pltpu.roll(to_e, LANES - step * t, 1)
        cot_d = to_d if cot_d is None else cot_d + to_d
        cot_e = to_e if cot_e is None else cot_e + to_e
    return cot_e, cot_d


def lane_of(rows):
    return lax.broadcasted_iota(jnp.int32, (rows, LANES), 1)


def slot_of(place, other, local):
    return lax.rem(other - place + local, local)


def came_in(place, other, local):
    return lax.rem(place - other + local, local)


def prepare_kernel(
    sk, sketch_ref, norm_ref, dnorm_ref, map_ref, states_ref, dstates_ref,
    fwd_ref, bwd_ref, wb_ref, ba_ref, bb_ref, rows_ref, state_ref, dstate_ref, done_ref,
):
    mine, half, _ = state_ref.shape
    own = pl.ds(lax.axis_index("local") * mine, mine)
    copies = [
        pltpu.make_async_copy(states_ref.at[own], state_ref, done_ref.at[0]),
        pltpu.make_async_copy(dstates_ref.at[own], dstate_ref, done_ref.at[1]),
    ]
    for copy in copies:
        copy.start()
    table = map_ref[...]
    step = LANES // sk
    left, right = sketch_ref[0], sketch_ref[1] * sk ** (-0.5)

    def turns(x):
        return [x] + [jnp.concatenate([x[j:], x[:j]], axis=0) for j in range(1, step)]

    full = jnp.concatenate([left] * step + [right] * step + turns(left) + turns(right), axis=0)
    hi, lo = split(full)
    none = jnp.zeros_like(full)
    ba_ref[...] = jnp.concatenate([hi.astype(F32), none], axis=1).astype(BF16)
    bb_ref[...] = jnp.concatenate([none, hi.astype(F32)], axis=1).astype(BF16)
    hi, lo = hi.astype(F32).T, lo.astype(F32).T
    none = jnp.zeros_like(hi)
    wb_ref[...] = jnp.concatenate([none, hi, none, lo], axis=0).astype(BF16)

    def mapped(x):
        hi, lo = split(x)
        return mm(hi, table) + mm(lo, table)

    for which, (s_ref, n_ref, o_ref, scale) in enumerate(
        ((state_ref, norm_ref, fwd_ref, 1.0), (dstate_ref, dnorm_ref, bwd_ref, 1.0 / half))
    ):
        rows_ref[which] = mapped(n_ref[...]) * scale
        copies[which].wait()
        for m in range(mine):
            o_ref[m, :half] = mapped(s_ref[m])
            o_ref[m, half:] = jnp.broadcast_to(
                rows_ref[which, pl.ds(lax.axis_index("local") * mine + m, 1), :], (LANES - half, o_ref.shape[2])
            )


def project_kernel(hd, local, count, *refs):
    pieces = refs[:count]
    weights = refs[count : count + 3]
    grad_ref = refs[count + 3]
    out_refs = refs[count + 4 : -1]
    blocks_ref = refs[-1]
    depth = pieces[0].shape[1]
    rows = pieces[0].shape[0]
    mine = blocks_ref.shape[1]
    sums = []
    for w in weights:
        total = None
        for i, x in enumerate(pieces):
            part = mm(x[...], w[pl.ds(pl.multiple_of(lax.bitwise_xor(lax.axis_index("head"), i) * depth, depth), depth), :])
            total = part if total is None else total + part
        sums.append(total)
    value, key, query = sums
    for h in range(local * mine):
        cols = slice(h * hd, (h + 1) * hd)
        slot = slot_of(lax.axis_index("local"), h // mine, local)
        blocks_ref[slot, h % mine, :rows] = jnp.concatenate([value[:, cols], key[:, cols]], axis=1).astype(BF16)
        blocks_ref[slot, h % mine, rows:] = jnp.concatenate(
            [grad_ref[:, cols].astype(F32), query[:, cols]], axis=1
        ).astype(BF16)
    for s, out_ref in enumerate(out_refs):
        out_ref[...] = blocks_ref[s]


def window_rows(hd, sk):
    tiles = tile_count(sk)
    return (tiles - 1) * hd + hd // (2 * LANES // sk) + 8


def pack_window(total, hd, sk):
    tiles = tile_count(sk)
    used = sk // 2
    short = hd // (LANES // used)
    lane = lane_of(short)
    row = lax.broadcasted_iota(jnp.int32, (8, LANES), 0)
    last = total[:hd, LANES * (tiles - 1) :]
    tail = jnp.zeros((short, LANES), F32)
    for i in range(LANES // used):
        part = last[short * i : short * (i + 1)]
        tail = jnp.where(lane // used == i, pltpu.roll(part, used * i, 1) if i else part, tail)
    sums = jnp.zeros((8, LANES), F32)
    for t in range(tiles):
        sums = jnp.where(row == t, total[hd : hd + 8, LANES * t : LANES * (t + 1)], sums)
    full = [total[:hd, LANES * t : LANES * (t + 1)] for t in range(tiles - 1)]
    return jnp.concatenate(full + [tail, sums], axis=0).astype(BF16)


def unpack_window(packed, hd, sk):
    tiles = tile_count(sk)
    used = sk // 2
    short = hd // (LANES // used)
    lane = lane_of(short)
    end = (tiles - 1) * hd
    rest = packed[end:].astype(F32)
    tail, sums = rest[:short], rest[short:]
    parts = []
    for i in range(LANES // used):
        part = jnp.where(lane < used, pltpu.roll(tail, LANES - used * i, 1) if i else tail, 0.0)
        parts.append(part + pltpu.roll(part, used, 1))
    last = jnp.concatenate(parts, axis=0).astype(BF16)
    state = jnp.concatenate([packed[hd * t : hd * (t + 1)] for t in range(tiles - 1)] + [last], axis=1)
    norm = jnp.concatenate(
        [jnp.broadcast_to(sums[t : t + 1], (16, LANES)) for t in range(tiles)], axis=1
    ).astype(BF16)
    return jnp.concatenate([state, norm], axis=0)


def key_kernel(sk, hd, local, *refs):
    slots = refs[:local]
    base_ref, wb_ref, qkv_ref, state_ref, feat_ref, kdot_ref, total_ref = refs[local:]
    blocks, mine, packed, _ = qkv_ref.shape
    for s, slot in enumerate(slots):
        qkv_ref[came_in(lax.axis_index("local"), s, blocks)] = slot[...]
    rows = packed // 2
    width = base_ref.shape[2]
    tiles = width // LANES
    weights = lane_weights(sk, width)
    lane = lane_of(rows)
    for m in range(mine):
        state = base_ref[m]
        for c in range(blocks):
            state_ref[m, c] = state.astype(BF16)
            vk = qkv_ref[c, m, :rows]
            e0, e1, d0, d1 = sketched(vk, wb_ref[...])
            e, d = e0 * e1, d0 * d1
            feat = features(e, d, sk, tiles)
            feat_ref[m, c] = feat
            hi, lo = split(e)
            kdot_ref[m, c] = jnp.where(
                lane < 2 * sk, hi.astype(F32), jnp.where(lane < 3 * sk, lo.astype(F32), 0.0)
            ).astype(BF16)
            ones = jnp.where(lane < hd, vk.astype(F32), 1.0).astype(BF16)
            state = state + mm(ones, feat, TN) * weights
        total_ref[m] = state


def query_kernel(
    sk, hd, qkv_ref, kdot_ref, state_ref, wb_ref, ba_ref, bb_ref,
    dq_ref, qdot_ref, dn_ref, cot_ref, total_ref,
):
    blocks, mine, packed, _ = qkv_ref.shape
    rows = packed // 2
    half = rows // 2
    width = state_ref.shape[3]
    tiles = width // LANES
    lane = lane_of(rows)
    low = lane < hd
    causal = lax.broadcasted_iota(jnp.int32, (rows, rows), 0) >= lax.broadcasted_iota(
        jnp.int32, (rows, rows), 1
    )
    r_i = lax.broadcasted_iota(jnp.int32, (2 * LANES, LANES), 0) % LANES
    c_i = lax.broadcasted_iota(jnp.int32, (2 * LANES, LANES), 1)
    adder = jnp.where((r_i < hd) & (c_i >= hd), -1.0 / (LANES - hd), 0.0).astype(BF16)
    for m in range(mine):
        total = jnp.zeros((LANES, width), F32)
        for c in range(blocks):
            gq = qkv_ref[c, m, rows:]
            e0, e1, d0, d1 = sketched(gq, wb_ref[...])
            e, d = e0 * e1, d0 * d1
            feat = features(e, d, sk, tiles)
            hi, lo = split(e)
            qdot = jnp.where(
                (lane >= sk) & (lane < 2 * sk),
                lo.astype(F32),
                jnp.where(lane < 3 * sk, hi.astype(F32), 0.0),
            ).astype(BF16)
            qdot_ref[m, c] = qdot
            kdot = kdot_ref[m, c]
            state = state_ref[m, c]
            ones = jnp.where(low, qkv_ref[c, m, :rows].astype(F32), 1.0).astype(BF16)
            dots = jnp.where(causal, mm(qdot, kdot, NT), 0.0)
            num = mm(feat, state, NT) + mm((dots * dots).astype(BF16), ones)
            inv = 1.0 / (1.0 + num)
            inv = jnp.where(low, pltpu.roll(inv, hd, 1), inv)
            g = gq.astype(F32)
            g_hi, g_lo = split(jnp.where(low, g * num, 0.0))
            den = mm(jnp.concatenate([g_hi, g_lo], axis=1), adder)
            dn = (jnp.where(low, g, den * inv) * inv).astype(BF16)
            dn_ref[m, c] = dn
            cot_dots = (2.0 * dots * mm(dn, ones, NT)).astype(BF16)
            near = mm(cot_dots, kdot)
            cot = mm(dn, state)
            cot_e, cot_d = feature_pull(cot, e, d, sk, tiles)
            cot_e = cot_e + jnp.where((lane < sk) | (lane >= 2 * sk), near, 0.0)
            back = jnp.concatenate(
                [
                    (cot_e * e1).astype(BF16),
                    (cot_e * e0).astype(BF16),
                    (cot_d * d1).astype(BF16),
                    (cot_d * d0).astype(BF16),
                ],
                axis=1,
            )
            dq_ref[m, c] = (mm(back[:half], ba_ref[...]) + mm(back[half:], bb_ref[...])).astype(BF16)
            here = mm(dn, feat, TN)
            cot_ref[m, c] = here
            total = total + here
        total_ref[m] = pack_window(total, hd, sk)


def reverse_kernel(
    sk, hd, window_ref, qkv_ref, dq_ref, feat_ref, kdot_ref, qdot_ref, dn_ref, cot_ref, base_ref, wb_ref, bb_ref, *refs
):
    out_refs = refs[:-1]
    blocks_ref = refs[-1]
    mine, blocks, rows, _ = dn_ref.shape
    packed = rows + rows // 2
    width = base_ref.shape[2]
    tiles = width // LANES
    weights = lane_weights(sk, width)
    lane = lane_of(rows)
    low = lane < hd
    causal = lax.broadcasted_iota(jnp.int32, (rows, rows), 0) <= lax.broadcasted_iota(
        jnp.int32, (rows, rows), 1
    )
    for m in range(mine):
        state = base_ref[m]
        for c in reversed(range(blocks)):
            after = state.astype(BF16)
            vk = qkv_ref[c, m, :rows]
            e0, e1, d0, d1 = sketched(vk, wb_ref[...])
            e, d = e0 * e1, d0 * d1
            qdot = qdot_ref[m, c]
            dn = dn_ref[m, c]
            ones = jnp.where(low, vk.astype(F32), 1.0).astype(BF16)
            dots = jnp.where(causal, mm(kdot_ref[m, c], qdot, NT), 0.0)
            cot_dots = (2.0 * dots * mm(ones, dn, NT)).astype(BF16)
            near = mm(cot_dots, qdot)
            dv = mm(feat_ref[m, c], after, NT) + mm((dots * dots).astype(BF16), dn)
            cot = mm(ones, after)
            cot_e, cot_d = feature_pull(cot, e, d, sk, tiles)
            cot_e = cot_e + jnp.where(lane < 2 * sk, near, 0.0)
            back = jnp.concatenate(
                [
                    (cot_e * e1).astype(BF16),
                    (cot_e * e0).astype(BF16),
                    (cot_d * d1).astype(BF16),
                    (cot_d * d0).astype(BF16),
                ],
                axis=1,
            )
            slot = slot_of(lax.axis_index("local"), c, blocks)
            blocks_ref[slot, m, :rows] = (jnp.where(low, dv, 0.0) + mm(back, bb_ref[...])).astype(BF16)
            blocks_ref[slot, m, rows:] = dq_ref[m, c]
            state = state + cot_ref[m, c] * weights
    for s, out_ref in enumerate(out_refs):
        out_ref[:, :packed] = blocks_ref[s]
        out_ref[:, packed:] = window_ref[...]


def input_kernel(hd, local, order, *refs):
    slots = refs[:local]
    weights = refs[local : local + 3]
    dq_ref, dk_ref, dv_ref, out_ref, all_ref = refs[local + 3 :]
    depth = dk_ref.shape[1]
    _, mine, packed, _ = all_ref.shape
    for s, slot in enumerate(slots):
        all_ref[came_in(lax.axis_index("local"), s, local)] = slot[:, :packed]
    rows = packed * 2 // 3
    half = rows // 2
    low = lane_of(rows) < hd

    def block(head):
        return all_ref[head // mine, head % mine].astype(F32)

    for pair in range(local * mine // 2):
        a, b = block(2 * pair), block(2 * pair + 1)
        cols = slice(pair * LANES, (pair + 1) * LANES)
        dv_ref[:, cols] = jnp.where(low, a[:rows], pltpu.roll(b[:rows], hd, 1)).astype(BF16)
        dk_ref[:, cols] = jnp.where(low, pltpu.roll(a[:rows], hd, 1), b[:rows]).astype(BF16)
        a, b = a[rows:], b[rows:]
        dq_ref[:half, cols] = jnp.where(low[:half], a, pltpu.roll(b, hd, 1)).astype(BF16)
        dq_ref[half:, cols] = jnp.where(low[:half], pltpu.roll(a, hd, 1), b).astype(BF16)
    dq, dk, dv = dq_ref[...], dk_ref[...], dv_ref[...]
    for i in range(out_ref.shape[0]):
        total = None
        for w, x in zip(weights, (dq, dk, dv)):
            part = mm(x, w[pl.ds(pl.multiple_of(lax.bitwise_xor(lax.axis_index("head"), order[i]) * depth, depth), depth), :], NT)
            total = part if total is None else total + part
        out_ref[i] = total.astype(BF16)


def expand_kernel(hd, sk, local, *refs):
    slots = refs[:local]
    dstate_ref, dnorm_ref, map_ref, state_ref, norm_ref, all_ref = refs[local:]
    mine = slots[0].shape[0]
    first = slots[0].shape[1] - window_rows(hd, sk)
    heads, rows, width = all_ref.shape
    for s, slot in enumerate(slots):
        for m in range(mine):
            all_ref[came_in(lax.axis_index("local"), s, local) * mine + m] = unpack_window(slot[m, first:], hd, sk)
    spread = mm(all_ref[...].reshape(heads * rows, width), map_ref[...], NT)
    for h in range(heads):
        state_ref[h] = dstate_ref[h] + spread[h * rows : h * rows + hd]
        norm_ref[h : h + 1] = dnorm_ref[h : h + 1] + spread[h * rows + hd : h * rows + hd + 1] * float(LANES - hd)


def call(kernel, name, out_shape, arrays, stay=(), mib=16, scratch=()):
    vmem = pl.BlockSpec(memory_space=pltpu.VMEM)
    return pl.pallas_call(
        kernel,
        in_specs=[vmem] * len(arrays) + [pl.BlockSpec(memory_space=pltpu.HBM)] * len(stay),
        out_specs=[vmem] * len(out_shape),
        out_shape=[jax.ShapeDtypeStruct(dims, kind) for dims, kind in out_shape],
        scratch_shapes=list(scratch),
        compiler_params=pltpu.CompilerParams(vmem_limit_bytes=mib * MIB),
        name=name,
    )(*arrays, *stay)


def hop(x, axis, distance):
    count = lax.axis_size(axis)
    return lax.ppermute(x, axis, [(i, i ^ distance) for i in range(count)])


def body(groups, local, inputs, w_query, w_key, w_value, sketch, prefix_state, prefix_norm, d_attn, d_state_end, d_norm_end):
    rows, depth = inputs.shape
    width = w_query.shape[1]
    heads, feat, hd = prefix_state.shape
    sk = sketch.shape[2]
    tiles = tile_count(sk)
    lanes = tiles * LANES
    half = rows // 2
    packed = rows + half
    mine = heads // local
    ranks = lax.axis_size("head")
    group = lax.axis_index("group")

    def send(x, shift):
        return lax.ppermute(x, "local", [(i, (i + shift) % local) for i in range(local)])

    def exchange(x):
        order = sorted(range(1, local), key=lambda s: -min(s, local - s))
        came = {s: send(x[s], s) for s in order}
        came[0] = x[0]
        return [came[s] for s in range(local)]

    pieces = {0: inputs}
    far = {ranks // 2: hop(inputs, "head", ranks // 2)} if ranks > 1 else {}

    table = jnp.asarray(pair_map(sk), BF16)

    state_t = prefix_state.transpose(0, 2, 1)
    dstate_t = d_state_end.transpose(0, 2, 1)
    base, base_after, wb, ba, bb = call(
        partial(prepare_kernel, sk),
        "prepare",
        [((mine, LANES, lanes), F32)] * 2 + [((4 * hd, 4 * LANES), BF16)] + [((4 * LANES, 2 * hd), BF16)] * 2,
        [sketch.transpose(0, 2, 1), prefix_norm, d_norm_end, table],
        [state_t, dstate_t],
        scratch=[
            pltpu.VMEM((2, heads, lanes), F32),
            pltpu.VMEM((mine, hd, feat), F32),
            pltpu.VMEM((mine, hd, feat), F32),
            pltpu.SemaphoreType.DMA((2,)),
        ],
    )
    far, base, base_after, wb, ba, bb = lax.optimization_barrier((far, base, base_after, wb, ba, bb))
    pieces.update(far)
    distance = ranks // 4
    while distance:
        pieces.update({at ^ distance: hop(x, "head", distance) for at, x in list(pieces.items())})
        distance //= 2
    keys = range(ranks)

    block = ((mine, 2 * rows, LANES), BF16)
    all_blocks = pltpu.VMEM((local,) + block[0], BF16)
    back_blocks = pltpu.VMEM((local, mine, packed, LANES), BF16)
    slots = call(
        partial(project_kernel, hd, local, len(keys)),
        "project",
        [block] * local,
        [pieces[at] for at in keys] + [w_value, w_key, w_query, d_attn],
        scratch=[all_blocks],
    )
    slots = exchange(slots)

    def key_side(start_state):
        return call(
            partial(key_kernel, sk, hd, local),
            "key_side",
            [
                ((local, mine, 2 * rows, LANES), BF16),
                ((mine, local, LANES, lanes), BF16),
                ((mine, local, rows, lanes), BF16),
                ((mine, local, rows, LANES), BF16),
                ((mine, LANES, lanes), F32),
            ],
            [*slots, start_state, wb],
        )

    def of_groups(x, wanted):
        everything = lax.all_gather(x.astype(BF16), "group").astype(F32)
        chosen = wanted(jnp.arange(groups))
        return jnp.where(chosen.reshape((groups,) + (1,) * x.ndim), everything, 0.0).sum(0)

    if groups > 1:
        sums = key_side(jnp.zeros_like(base))[4]
        base = base + of_groups(sums, lambda at: at < group)
    qkv, states, key_feats, kdot, _ = key_side(base)

    dq, qdot, dn, cots, window = call(
        partial(query_kernel, sk, hd),
        "query_side",
        [
            ((mine, local, half, LANES), BF16),
            ((mine, local, rows, LANES), BF16),
            ((mine, local, rows, LANES), BF16),
            ((mine, local, LANES, lanes), F32),
            ((mine, window_rows(hd, sk), LANES), BF16),
        ],
        [qkv, kdot, states, wb, ba, bb],
    )
    if groups > 1:
        later = of_groups(cots.sum(1), lambda at: at > group)
        base_after = base_after + later * lane_weights(sk, lanes)

    if groups > 1:
        window = lax.psum(window, "group")
    gradients = call(
        partial(reverse_kernel, sk, hd),
        "key_gradients",
        [((mine, packed + window_rows(hd, sk), LANES), BF16)] * local,
        [window, qkv, dq, key_feats, kdot, qdot, dn, cots, base_after, wb, bb],
        scratch=[back_blocks],
    )
    gradients = exchange(gradients)

    order = sorted(range(ranks), key=lambda at: [-(at >> bit & 1) for bit in range(ranks.bit_length() - 1)])
    d_query, d_key, d_value, sums = call(
        partial(input_kernel, hd, local, order),
        "input_gradient",
        [((rows, width), BF16)] * 3 + [((ranks, rows, depth), BF16)],
        [*gradients, w_query, w_key, w_value],
        scratch=[back_blocks],
    )
    distance = 1
    while distance < ranks:
        count = sums.shape[0] // 2
        came = hop(sums[:count], "head", distance)
        sums = (sums[count:].astype(F32) + came.astype(F32)).astype(BF16)
        distance *= 2

    state_out, d_prefix_norm = call(
        partial(expand_kernel, hd, sk, local),
        "prefix_gradients",
        [((heads, hd, feat), F32), ((heads, feat), F32)],
        [*gradients, dstate_t, d_norm_end, table],
        scratch=[pltpu.VMEM((heads, hd + 16, lanes), BF16)],
    )
    d_prefix_state = state_out.transpose(0, 2, 1)
    return sums[0], d_query, d_key, d_value, d_prefix_state, d_prefix_norm


def solution(mesh):
    seq, head = mesh.shape["seq"], mesh.shape["head"]

    def run(*args):
        heads = args[5].shape[0] // head
        local = math.gcd(heads, seq)
        groups = seq // local
        inner = Mesh(mesh.devices.reshape(groups, local, head), ("group", "local", "head"))
        tokens = ("group", "local")
        return jax.shard_map(
            partial(body, groups, local),
            mesh=inner,
            in_specs=(
                P(tokens, "head"),
                P(None, "head"),
                P(None, "head"),
                P(None, "head"),
                P(),
                P("head", None, None),
                P("head", None),
                P(tokens, "head"),
                P("head", None, None),
                P("head", None),
            ),
            out_specs=(
                P(tokens, "head"),
                P(tokens, "head"),
                P(tokens, "head"),
                P(tokens, "head"),
                P("head", None, None),
                P("head", None),
            ),
            check_vma=False,
        )(*args)

    return run
```

```python
import math
from functools import partial

import jax
import jax.numpy as jnp
import numpy as np
from jax import lax
from jax.experimental import pallas as pl
from jax.experimental.pallas import tpu as pltpu
from jax.sharding import Mesh, PartitionSpec as P

F32 = jnp.float32
BF16 = jnp.bfloat16
LANES = 128
VMEM = pltpu.VMEM
MIB = 1024 * 1024
GROUP = 4

NN = (((1,), (0,)), ((), ()))
NT = (((1,), (1,)), ((), ()))
TN = (((0,), (0,)), ((), ()))


def mm(a, b, dims=NN):
    return lax.dot_general(a, b, dims, preferred_element_type=F32)


def split(x):
    hi = x.astype(BF16)
    return hi, (x - hi.astype(F32)).astype(BF16)


def tile_count(sk):
    return -(-(sk // 2 + 1) // (LANES // sk))


def pair_map(sk):
    step = LANES // sk
    width = tile_count(sk) * LANES
    lane = np.arange(width)
    tile, within = lane // LANES, lane % LANES
    j, a = within // sk, within % sk
    first, second = (a + j) % sk, (a - step * tile) % sk
    keep = step * tile + j <= sk // 2
    table = np.zeros((sk * sk, width), np.float32)
    for one in lane[keep]:
        x, y = first[one], second[one]
        r = step * tile[one] + j[one]
        if r == 0:
            table[x * sk + y, one] = 1.0
        else:
            value = 0.5 if 2 * r == sk else 1.0
            table[x * sk + y, one] = value
            table[y * sk + x, one] = value
    return table


def lane_weights(sk, width):
    lane = lax.broadcasted_iota(jnp.int32, (1, width), 1)
    r = (LANES // sk) * (lane // LANES) + (lane % LANES) // sk
    return jnp.where(
        r <= sk // 2, jnp.where((r == 0) | (2 * r == sk), 1.0, 2.0), 0.0
    ).astype(F32)


def sketched(x, weights):
    both = mm(jnp.concatenate([x, x], axis=1), weights)
    return tuple(both[:, LANES * i : LANES * (i + 1)] for i in range(4))


def turned(e, sk, tiles):
    step = LANES // sk
    return [e] + [pltpu.roll(e, step * t, 1) for t in range(1, tiles)]


def features(e, d, sk, tiles):
    return jnp.concatenate([(d * x).astype(BF16) for x in turned(e, sk, tiles)], axis=1)


def feature_pull(cot, e, d, sk, tiles):
    step = LANES // sk
    cot_e = cot_d = None
    for t, x in enumerate(turned(e, sk, tiles)):
        part = cot[:, LANES * t : LANES * (t + 1)]
        to_d = part * x
        to_e = part * d
        if t:
            to_e = pltpu.roll(to_e, LANES - step * t, 1)
        cot_d = to_d if cot_d is None else cot_d + to_d
        cot_e = to_e if cot_e is None else cot_e + to_e
    return cot_e, cot_d


def lane_of(rows):
    return lax.broadcasted_iota(jnp.int32, (rows, LANES), 1)


def slot_of(place, other, local):
    return lax.rem(other - place + local, local)


def came_in(place, other, local):
    return lax.rem(place - other + local, local)


def prepare_kernel(
    sk, sketch_ref, norm_ref, dnorm_ref, map_ref, states_ref, dstates_ref,
    fwd_ref, bwd_ref, wb_ref, ba_ref, bb_ref, rows_ref, state_ref, dstate_ref, done_ref,
):
    mine, half, _ = state_ref.shape
    own = pl.ds(lax.axis_index("local") * mine, mine)
    copies = [
        pltpu.make_async_copy(states_ref.at[own], state_ref, done_ref.at[0]),
        pltpu.make_async_copy(dstates_ref.at[own], dstate_ref, done_ref.at[1]),
    ]
    for copy in copies:
        copy.start()
    table = map_ref[...]
    step = LANES // sk
    left, right = sketch_ref[0], sketch_ref[1] * sk ** (-0.5)

    def turns(x):
        return [x] + [jnp.concatenate([x[j:], x[:j]], axis=0) for j in range(1, step)]

    full = jnp.concatenate([left] * step + [right] * step + turns(left) + turns(right), axis=0)
    hi, lo = split(full)
    none = jnp.zeros_like(full)
    ba_ref[...] = jnp.concatenate([hi.astype(F32), none], axis=1).astype(BF16)
    bb_ref[...] = jnp.concatenate([none, hi.astype(F32)], axis=1).astype(BF16)
    hi, lo = hi.astype(F32).T, lo.astype(F32).T
    none = jnp.zeros_like(hi)
    wb_ref[...] = jnp.concatenate([none, hi, none, lo], axis=0).astype(BF16)

    def mapped(x):
        hi, lo = split(x)
        return mm(hi, table) + mm(lo, table)

    for which, (s_ref, n_ref, o_ref, scale) in enumerate(
        ((state_ref, norm_ref, fwd_ref, 1.0), (dstate_ref, dnorm_ref, bwd_ref, 1.0 / half))
    ):
        rows_ref[which] = mapped(n_ref[...]) * scale
        copies[which].wait()
        for m in range(mine):
            o_ref[m, :half] = mapped(s_ref[m])
            o_ref[m, half:] = jnp.broadcast_to(
                rows_ref[which, pl.ds(lax.axis_index("local") * mine + m, 1), :], (LANES - half, o_ref.shape[2])
            )


def load_kernel(count, *refs):
    sources, targets, done_ref = refs[:count], refs[count:-1], refs[-1]
    copies = [
        pltpu.make_async_copy(source, target, done_ref.at[i]) for i, (source, target) in enumerate(zip(sources, targets))
    ]
    for copy in copies:
        copy.start()
    for copy in copies:
        copy.wait()


def project_kernel(hd, local, count, *refs):
    pieces = refs[:count]
    weights = refs[count : count + 3]
    grad_ref = refs[count + 3]
    out_refs = refs[count + 4 : -1]
    blocks_ref = refs[-1]
    depth = pieces[0].shape[1]
    rows = pieces[0].shape[0]
    mine = blocks_ref.shape[1]
    sums = []
    for w in weights:
        total = None
        for i, x in enumerate(pieces):
            part = mm(x[...], w[pl.ds(pl.multiple_of(lax.bitwise_xor(lax.axis_index("head"), i) * depth, depth), depth), :])
            total = part if total is None else total + part
        sums.append(total)
    value, key, query = sums
    for h in range(local * mine):
        cols = slice(h * hd, (h + 1) * hd)
        slot = slot_of(lax.axis_index("local"), h // mine, local)
        blocks_ref[slot, h % mine, :rows] = jnp.concatenate([value[:, cols], key[:, cols]], axis=1).astype(BF16)
        blocks_ref[slot, h % mine, rows:] = jnp.concatenate(
            [grad_ref[:, cols].astype(F32), query[:, cols]], axis=1
        ).astype(BF16)
    for s, out_ref in enumerate(out_refs):
        out_ref[...] = blocks_ref[s]


def window_rows(hd, sk):
    tiles = tile_count(sk)
    return (tiles - 1) * hd + hd // (2 * LANES // sk) + 8


def pack_window(total, hd, sk):
    tiles = tile_count(sk)
    used = sk // 2
    short = hd // (LANES // used)
    lane = lane_of(short)
    row = lax.broadcasted_iota(jnp.int32, (8, LANES), 0)
    last = total[:hd, LANES * (tiles - 1) :]
    tail = jnp.zeros((short, LANES), F32)
    for i in range(LANES // used):
        part = last[short * i : short * (i + 1)]
        tail = jnp.where(lane // used == i, pltpu.roll(part, used * i, 1) if i else part, tail)
    sums = jnp.zeros((8, LANES), F32)
    for t in range(tiles):
        sums = jnp.where(row == t, total[hd : hd + 8, LANES * t : LANES * (t + 1)], sums)
    full = [total[:hd, LANES * t : LANES * (t + 1)] for t in range(tiles - 1)]
    return jnp.concatenate(full + [tail, sums], axis=0).astype(BF16)


def unpack_window(packed, hd, sk):
    tiles = tile_count(sk)
    used = sk // 2
    short = hd // (LANES // used)
    lane = lane_of(short)
    end = (tiles - 1) * hd
    rest = packed[end:].astype(F32)
    tail, sums = rest[:short], rest[short:]
    parts = []
    for i in range(LANES // used):
        part = jnp.where(lane < used, pltpu.roll(tail, LANES - used * i, 1) if i else tail, 0.0)
        parts.append(part + pltpu.roll(part, used, 1))
    last = jnp.concatenate(parts, axis=0).astype(BF16)
    state = jnp.concatenate([packed[hd * t : hd * (t + 1)] for t in range(tiles - 1)] + [last], axis=1)
    norm = jnp.concatenate(
        [jnp.broadcast_to(sums[t : t + 1], (16, LANES)) for t in range(tiles)], axis=1
    ).astype(BF16)
    return jnp.concatenate([state, norm], axis=0)


def whole_state(packed, hd, sk):
    both = unpack_window(packed, hd, sk).astype(F32)
    return jnp.concatenate([both[:hd]] + [both[hd:]] * ((LANES - hd) // 16), axis=0)


def key_kernel(sk, hd, local, *refs):
    slots = refs[:local]
    wb_ref, qkv_ref, state_ref, feat_ref, kdot_ref, total_ref = refs[local:]
    blocks, mine, packed, _ = qkv_ref.shape
    for s, slot in enumerate(slots):
        qkv_ref[came_in(lax.axis_index("local"), s, blocks)] = slot[...]
    rows = packed // 2
    width = state_ref.shape[3]
    tiles = width // LANES
    weights = lane_weights(sk, width)
    lane = lane_of(rows)
    for m in range(mine):
        state = jnp.zeros((LANES, width), F32)
        for c in range(blocks):
            state_ref[m, c] = state
            vk = qkv_ref[c, m, :rows]
            e0, e1, d0, d1 = sketched(vk, wb_ref[...])
            e, d = e0 * e1, d0 * d1
            feat = features(e, d, sk, tiles)
            feat_ref[m, c] = feat
            hi, lo = split(e)
            kdot_ref[m, c] = jnp.where(
                lane < 2 * sk, hi.astype(F32), jnp.where(lane < 3 * sk, lo.astype(F32), 0.0)
            ).astype(BF16)
            ones = jnp.where(lane < hd, vk.astype(F32), 1.0).astype(BF16)
            state = state + mm(ones, feat, TN) * weights
        total_ref[m] = pack_window(state, hd, sk)


def query_kernel(
    sk, hd, carry_ref, base_ref, qkv_ref, kdot_ref, state_ref, wb_ref, ba_ref, bb_ref,
    dq_ref, qdot_ref, dn_ref, cot_ref, total_ref,
):
    blocks, mine, packed, _ = qkv_ref.shape
    rows = packed // 2
    half = rows // 2
    width = state_ref.shape[3]
    tiles = width // LANES
    lane = lane_of(rows)
    low = lane < hd
    causal = lax.broadcasted_iota(jnp.int32, (rows, rows), 0) >= lax.broadcasted_iota(
        jnp.int32, (rows, rows), 1
    )
    r_i = lax.broadcasted_iota(jnp.int32, (2 * LANES, LANES), 0) % LANES
    c_i = lax.broadcasted_iota(jnp.int32, (2 * LANES, LANES), 1)
    adder = jnp.where((r_i < hd) & (c_i >= hd), -1.0 / (LANES - hd), 0.0).astype(BF16)
    for m in range(mine):
        total = jnp.zeros((LANES, width), F32)
        base = base_ref[m] if carry_ref is None else base_ref[m] + whole_state(carry_ref[m], hd, sk)
        for c in range(blocks):
            gq = qkv_ref[c, m, rows:]
            e0, e1, d0, d1 = sketched(gq, wb_ref[...])
            e, d = e0 * e1, d0 * d1
            feat = features(e, d, sk, tiles)
            hi, lo = split(e)
            qdot = jnp.where(
                (lane >= sk) & (lane < 2 * sk),
                lo.astype(F32),
                jnp.where(lane < 3 * sk, hi.astype(F32), 0.0),
            ).astype(BF16)
            qdot_ref[m, c] = qdot
            kdot = kdot_ref[m, c]
            state = (base + state_ref[m, c]).astype(BF16)
            ones = jnp.where(low, qkv_ref[c, m, :rows].astype(F32), 1.0).astype(BF16)
            dots = jnp.where(causal, mm(qdot, kdot, NT), 0.0)
            num = mm(feat, state, NT) + mm((dots * dots).astype(BF16), ones)
            inv = 1.0 / (1.0 + num)
            inv = jnp.where(low, pltpu.roll(inv, hd, 1), inv)
            g = gq.astype(F32)
            g_hi, g_lo = split(jnp.where(low, g * num, 0.0))
            den = mm(jnp.concatenate([g_hi, g_lo], axis=1), adder)
            dn = (jnp.where(low, g, den * inv) * inv).astype(BF16)
            dn_ref[m, c] = dn
            cot_dots = (2.0 * dots * mm(dn, ones, NT)).astype(BF16)
            near = mm(cot_dots, kdot)
            cot = mm(dn, state)
            cot_e, cot_d = feature_pull(cot, e, d, sk, tiles)
            cot_e = cot_e + jnp.where((lane < sk) | (lane >= 2 * sk), near, 0.0)
            back = jnp.concatenate(
                [
                    (cot_e * e1).astype(BF16),
                    (cot_e * e0).astype(BF16),
                    (cot_d * d1).astype(BF16),
                    (cot_d * d0).astype(BF16),
                ],
                axis=1,
            )
            dq_ref[m, c] = (mm(back[:half], ba_ref[...]) + mm(back[half:], bb_ref[...])).astype(BF16)
            here = mm(dn, feat, TN)
            cot_ref[m, c] = here
            total = total + here
        total_ref[m] = pack_window(total, hd, sk)


def reverse_kernel(
    sk, hd, others, window_ref, qkv_ref, dq_ref, feat_ref, kdot_ref, qdot_ref, dn_ref, cot_ref, base_ref, wb_ref, bb_ref, *refs
):
    other_refs = refs[:others]
    out_refs = refs[others:-1]
    blocks_ref = refs[-1]
    window, later = window_ref[...].astype(F32), None
    for d, other_ref in enumerate(other_refs, 1):
        other = other_ref[...].astype(F32)
        window = window + other
        other = jnp.where(lax.axis_index("group") < d, other, 0.0)
        later = other if later is None else later + other
    window = window.astype(BF16)
    mine, blocks, rows, _ = dn_ref.shape
    packed = rows + rows // 2
    width = base_ref.shape[2]
    tiles = width // LANES
    weights = lane_weights(sk, width)
    lane = lane_of(rows)
    low = lane < hd
    causal = lax.broadcasted_iota(jnp.int32, (rows, rows), 0) <= lax.broadcasted_iota(
        jnp.int32, (rows, rows), 1
    )
    for m in range(mine):
        state = base_ref[m]
        if later is not None:
            state = state + whole_state(later[m].astype(BF16), hd, sk) * weights
        for c in reversed(range(blocks)):
            after = state.astype(BF16)
            vk = qkv_ref[c, m, :rows]
            e0, e1, d0, d1 = sketched(vk, wb_ref[...])
            e, d = e0 * e1, d0 * d1
            qdot = qdot_ref[m, c]
            dn = dn_ref[m, c]
            ones = jnp.where(low, vk.astype(F32), 1.0).astype(BF16)
            dots = jnp.where(causal, mm(kdot_ref[m, c], qdot, NT), 0.0)
            cot_dots = (2.0 * dots * mm(ones, dn, NT)).astype(BF16)
            near = mm(cot_dots, qdot)
            dv = mm(feat_ref[m, c], after, NT) + mm((dots * dots).astype(BF16), dn)
            cot = mm(ones, after)
            cot_e, cot_d = feature_pull(cot, e, d, sk, tiles)
            cot_e = cot_e + jnp.where(lane < 2 * sk, near, 0.0)
            back = jnp.concatenate(
                [
                    (cot_e * e1).astype(BF16),
                    (cot_e * e0).astype(BF16),
                    (cot_d * d1).astype(BF16),
                    (cot_d * d0).astype(BF16),
                ],
                axis=1,
            )
            slot = slot_of(lax.axis_index("local"), c, blocks)
            blocks_ref[slot, m, :rows] = (jnp.where(low, dv, 0.0) + mm(back, bb_ref[...])).astype(BF16)
            blocks_ref[slot, m, rows:] = dq_ref[m, c]
            state = state + cot_ref[m, c] * weights
    for s, out_ref in enumerate(out_refs):
        out_ref[:, :packed] = blocks_ref[s]
        out_ref[:, packed:] = window


def input_kernel(hd, local, order, *refs):
    slots = refs[:local]
    weights = refs[local : local + 3]
    dq_ref, dk_ref, dv_ref, out_ref, all_ref = refs[local + 3 :]
    depth = dk_ref.shape[1]
    _, mine, packed, _ = all_ref.shape
    for s, slot in enumerate(slots):
        all_ref[came_in(lax.axis_index("local"), s, local)] = slot[:, :packed]
    rows = packed * 2 // 3
    half = rows // 2
    low = lane_of(rows) < hd

    def block(head):
        return all_ref[head // mine, head % mine].astype(F32)

    for pair in range(local * mine // 2):
        a, b = block(2 * pair), block(2 * pair + 1)
        cols = slice(pair * LANES, (pair + 1) * LANES)
        dv_ref[:, cols] = jnp.where(low, a[:rows], pltpu.roll(b[:rows], hd, 1)).astype(BF16)
        dk_ref[:, cols] = jnp.where(low, pltpu.roll(a[:rows], hd, 1), b[:rows]).astype(BF16)
        a, b = a[rows:], b[rows:]
        dq_ref[:half, cols] = jnp.where(low[:half], a, pltpu.roll(b, hd, 1)).astype(BF16)
        dq_ref[half:, cols] = jnp.where(low[:half], pltpu.roll(a, hd, 1), b).astype(BF16)
    dq, dk, dv = dq_ref[...], dk_ref[...], dv_ref[...]
    for i in range(out_ref.shape[0]):
        total = None
        for w, x in zip(weights, (dq, dk, dv)):
            part = mm(x, w[pl.ds(pl.multiple_of(lax.bitwise_xor(lax.axis_index("head"), order[i]) * depth, depth), depth), :], NT)
            total = part if total is None else total + part
        out_ref[i] = total.astype(BF16)


def expand_kernel(hd, sk, local, *refs):
    slots = refs[:local]
    dstate_ref, dnorm_ref, map_ref, state_ref, norm_ref, all_ref = refs[local:]
    mine = slots[0].shape[0]
    first = slots[0].shape[1] - window_rows(hd, sk)
    heads, rows, width = all_ref.shape
    for s, slot in enumerate(slots):
        for m in range(mine):
            all_ref[came_in(lax.axis_index("local"), s, local) * mine + m] = unpack_window(slot[m, first:], hd, sk)
    spread = mm(all_ref[...].reshape(heads * rows, width), map_ref[...], NT)
    for h in range(heads):
        state_ref[h] = dstate_ref[h] + spread[h * rows : h * rows + hd]
        norm_ref[h : h + 1] = dnorm_ref[h : h + 1] + spread[h * rows + hd : h * rows + hd + 1] * float(LANES - hd)


def call(kernel, name, out_shape, arrays, stay=(), mib=16, scratch=()):
    vmem = pl.BlockSpec(memory_space=pltpu.VMEM)
    return pl.pallas_call(
        kernel,
        in_specs=[vmem] * len(arrays) + [pl.BlockSpec(memory_space=pltpu.HBM)] * len(stay),
        out_specs=[vmem] * len(out_shape),
        out_shape=[jax.ShapeDtypeStruct(dims, kind) for dims, kind in out_shape],
        scratch_shapes=list(scratch),
        compiler_params=pltpu.CompilerParams(vmem_limit_bytes=mib * MIB),
        name=name,
    )(*arrays, *stay)


def hop(x, axis, distance):
    count = lax.axis_size(axis)
    return lax.ppermute(x, axis, [(i, i ^ distance) for i in range(count)])


def body(groups, local, inputs, w_query, w_key, w_value, sketch, prefix_state, prefix_norm, d_attn, d_state_end, d_norm_end):
    rows, depth = inputs.shape
    width = w_query.shape[1]
    heads, feat, hd = prefix_state.shape
    sk = sketch.shape[2]
    tiles = tile_count(sk)
    lanes = tiles * LANES
    half = rows // 2
    packed = rows + half
    mine = heads // local
    ranks = lax.axis_size("head")
    group = lax.axis_index("group")

    def send(x, shift):
        return lax.ppermute(x, "local", [(i, (i + shift) % local) for i in range(local)])

    def exchange(x):
        order = sorted(range(1, local), key=lambda s: -min(s, local - s))
        came = {s: send(x[s], s) for s in order}
        came[0] = x[0]
        return [came[s] for s in range(local)]

    pieces = {0: inputs}
    far = {ranks // 2: hop(inputs, "head", ranks // 2)} if ranks > 1 else {}

    table = jnp.asarray(pair_map(sk), BF16)

    state_t = prefix_state.transpose(0, 2, 1)
    dstate_t = d_state_end.transpose(0, 2, 1)
    loads = (w_value, w_key, w_query, d_attn, inputs)
    loaded = call(
        partial(load_kernel, len(loads)),
        "load",
        [(x.shape, x.dtype) for x in loads],
        [],
        loads,
        mib=48,
        scratch=[pltpu.SemaphoreType.DMA((len(loads),))],
    )
    far, loaded = lax.optimization_barrier((far, list(loaded)))
    pieces.update(far)
    distance = ranks // 4
    while distance:
        pieces.update({at ^ distance: hop(x, "head", distance) for at, x in list(pieces.items())})
        distance //= 2
    keys = list(range(ranks))

    block = ((mine, 2 * rows, LANES), BF16)
    all_blocks = pltpu.VMEM((local,) + block[0], BF16)
    back_blocks = pltpu.VMEM((local, mine, packed, LANES), BF16)
    slots = call(
        partial(project_kernel, hd, local, len(keys)),
        "project",
        [block] * local,
        [loaded[4]] + [pieces[at] for at in keys[1:]] + loaded[:4],
        scratch=[all_blocks],
    )
    sketch, first = lax.optimization_barrier((sketch, slots[0]))
    slots = exchange([first, *slots[1:]])
    base, base_after, wb, ba, bb = call(
        partial(prepare_kernel, sk),
        "prepare",
        [((mine, LANES, lanes), F32)] * 2 + [((4 * hd, 4 * LANES), BF16)] + [((4 * LANES, 2 * hd), BF16)] * 2,
        [sketch.transpose(0, 2, 1), prefix_norm, d_norm_end, table],
        [state_t, dstate_t],
        scratch=[
            pltpu.VMEM((2, heads, lanes), F32),
            pltpu.VMEM((mine, hd, feat), F32),
            pltpu.VMEM((mine, hd, feat), F32),
            pltpu.SemaphoreType.DMA((2,)),
        ],
    )

    small = ((mine, window_rows(hd, sk), LANES), BF16)
    qkv, states, key_feats, kdot, total = call(
        partial(key_kernel, sk, hd, local),
        "key_side",
        [
            ((local, mine, 2 * rows, LANES), BF16),
            ((mine, local, LANES, lanes), F32),
            ((mine, local, rows, lanes), BF16),
            ((mine, local, rows, LANES), BF16),
            small,
        ],
        [*slots, wb],
    )

    carry = []
    for d in range(1, groups):
        carry.append(lax.ppermute(total, "group", [(i, i + d) for i in range(groups - d)]))
    carry = carry[:1] if len(carry) < 2 else [sum(x.astype(F32) for x in carry).astype(BF16)]
    side = partial(query_kernel, sk, hd) if carry else partial(query_kernel, sk, hd, None)
    dq, qdot, dn, cots, window = call(
        side,
        "query_side",
        [
            ((mine, local, half, LANES), BF16),
            ((mine, local, rows, LANES), BF16),
            ((mine, local, rows, LANES), BF16),
            ((mine, local, LANES, lanes), F32),
            small,
        ],
        [*carry, base, qkv, kdot, states, wb, ba, bb],
    )

    others = [lax.ppermute(window, "group", [(i, (i + d) % groups) for i in range(groups)]) for d in range(1, groups)]
    gradients = call(
        partial(reverse_kernel, sk, hd, len(others)),
        "key_gradients",
        [((mine, packed + window_rows(hd, sk), LANES), BF16)] * local,
        [window, qkv, dq, key_feats, kdot, qdot, dn, cots, base_after, wb, bb, *others],
        scratch=[back_blocks],
    )
    gradients = exchange(gradients)

    order = sorted(range(ranks), key=lambda at: [-(at >> bit & 1) for bit in range(ranks.bit_length() - 1)])
    d_query, d_key, d_value, sums = call(
        partial(input_kernel, hd, local, order),
        "input_gradient",
        [((rows, width), BF16)] * 3 + [((ranks, rows, depth), BF16)],
        [*gradients, w_query, w_key, w_value],
        scratch=[back_blocks],
    )
    distance = 1
    while distance < ranks:
        count = sums.shape[0] // 2
        came = hop(sums[:count], "head", distance)
        sums = (sums[count:].astype(F32) + came.astype(F32)).astype(BF16)
        distance *= 2

    state_out, d_prefix_norm = call(
        partial(expand_kernel, hd, sk, local),
        "prefix_gradients",
        [((heads, hd, feat), F32), ((heads, feat), F32)],
        [*gradients, dstate_t, d_norm_end, table],
        scratch=[pltpu.VMEM((heads, hd + 16, lanes), BF16)],
    )
    d_prefix_state = state_out.transpose(0, 2, 1)
    return sums[0], d_query, d_key, d_value, d_prefix_state, d_prefix_norm


def solution(mesh):
    seq, head = mesh.shape["seq"], mesh.shape["head"]

    def run(*args):
        heads = args[5].shape[0] // head
        local = math.gcd(heads, seq)
        local = min(local & -local, GROUP)
        groups = seq // local
        inner = Mesh(mesh.devices.reshape(groups, local, head), ("group", "local", "head"))
        tokens = ("group", "local")
        return jax.shard_map(
            partial(body, groups, local),
            mesh=inner,
            in_specs=(
                P(tokens, "head"),
                P(None, "head"),
                P(None, "head"),
                P(None, "head"),
                P(),
                P("head", None, None),
                P("head", None),
                P(tokens, "head"),
                P("head", None, None),
                P("head", None),
            ),
            out_specs=(
                P(tokens, "head"),
                P(tokens, "head"),
                P(tokens, "head"),
                P(tokens, "head"),
                P("head", None, None),
                P("head", None),
            ),
            check_vma=False,
        )(*args)

    return run
```

```python
import math
from functools import partial

import jax
import jax.numpy as jnp
import numpy as np
from jax import lax
from jax.experimental import pallas as pl
from jax.experimental.pallas import tpu as pltpu
from jax.sharding import Mesh, PartitionSpec as P

F32 = jnp.float32
BF16 = jnp.bfloat16
LANES = 128
VMEM = pltpu.VMEM
MIB = 1024 * 1024
GROUP = 4

NN = (((1,), (0,)), ((), ()))
NT = (((1,), (1,)), ((), ()))
TN = (((0,), (0,)), ((), ()))


def mm(a, b, dims=NN):
    return lax.dot_general(a, b, dims, preferred_element_type=F32)


def split(x):
    hi = x.astype(BF16)
    return hi, (x - hi.astype(F32)).astype(BF16)


def tile_count(sk):
    return -(-(sk // 2 + 1) // (LANES // sk))


def pair_map(sk):
    step = LANES // sk
    width = tile_count(sk) * LANES
    lane = np.arange(width)
    tile, within = lane // LANES, lane % LANES
    j, a = within // sk, within % sk
    first, second = (a + j) % sk, (a - step * tile) % sk
    keep = step * tile + j <= sk // 2
    table = np.zeros((sk * sk, width), np.float32)
    for one in lane[keep]:
        x, y = first[one], second[one]
        r = step * tile[one] + j[one]
        if r == 0:
            table[x * sk + y, one] = 1.0
        else:
            value = 0.5 if 2 * r == sk else 1.0
            table[x * sk + y, one] = value
            table[y * sk + x, one] = value
    return table


def lane_weights(sk, width):
    lane = lax.broadcasted_iota(jnp.int32, (1, width), 1)
    r = (LANES // sk) * (lane // LANES) + (lane % LANES) // sk
    return jnp.where(
        r <= sk // 2, jnp.where((r == 0) | (2 * r == sk), 1.0, 2.0), 0.0
    ).astype(F32)


def sketched(x, weights):
    both = mm(jnp.concatenate([x, x], axis=1), weights)
    return tuple(both[:, LANES * i : LANES * (i + 1)] for i in range(4))


def turned(e, sk, tiles):
    step = LANES // sk
    return [e] + [pltpu.roll(e, step * t, 1) for t in range(1, tiles)]


def features(e, d, sk, tiles):
    return jnp.concatenate([(d * x).astype(BF16) for x in turned(e, sk, tiles)], axis=1)


def feature_pull(cot, e, d, sk, tiles):
    step = LANES // sk
    cot_e = cot_d = None
    for t, x in enumerate(turned(e, sk, tiles)):
        part = cot[:, LANES * t : LANES * (t + 1)]
        to_d = part * x
        to_e = part * d
        if t:
            to_e = pltpu.roll(to_e, LANES - step * t, 1)
        cot_d = to_d if cot_d is None else cot_d + to_d
        cot_e = to_e if cot_e is None else cot_e + to_e
    return cot_e, cot_d


def lane_of(rows):
    return lax.broadcasted_iota(jnp.int32, (rows, LANES), 1)


def slot_of(place, other, local):
    return lax.rem(other - place + local, local)


def came_in(place, other, local):
    return lax.rem(place - other + local, local)


def prepare_kernel(
    sk, sketch_ref, norm_ref, dnorm_ref, map_ref, states_ref, dstates_ref,
    fwd_ref, bwd_ref, wb_ref, ba_ref, bb_ref, rows_ref, state_ref, dstate_ref, done_ref,
):
    mine, half, _ = state_ref.shape
    own = pl.ds(lax.axis_index("local") * mine, mine)
    copies = [
        pltpu.make_async_copy(states_ref.at[own], state_ref, done_ref.at[0]),
        pltpu.make_async_copy(dstates_ref.at[own], dstate_ref, done_ref.at[1]),
    ]
    for copy in copies:
        copy.start()
    table = map_ref[...]
    step = LANES // sk
    left, right = sketch_ref[0], sketch_ref[1] * sk ** (-0.5)

    def turns(x):
        return [x] + [jnp.concatenate([x[j:], x[:j]], axis=0) for j in range(1, step)]

    full = jnp.concatenate([left] * step + [right] * step + turns(left) + turns(right), axis=0)
    hi, lo = split(full)
    none = jnp.zeros_like(full)
    ba_ref[...] = jnp.concatenate([hi.astype(F32), none], axis=1).astype(BF16)
    bb_ref[...] = jnp.concatenate([none, hi.astype(F32)], axis=1).astype(BF16)
    hi, lo = hi.astype(F32).T, lo.astype(F32).T
    none = jnp.zeros_like(hi)
    wb_ref[...] = jnp.concatenate([none, hi, none, lo], axis=0).astype(BF16)

    def mapped(x):
        hi, lo = split(x)
        return mm(hi, table) + mm(lo, table)

    for which, (s_ref, n_ref, o_ref, scale) in enumerate(
        ((state_ref, norm_ref, fwd_ref, 1.0), (dstate_ref, dnorm_ref, bwd_ref, 1.0 / half))
    ):
        rows_ref[which] = mapped(n_ref[...]) * scale
        copies[which].wait()
        for m in range(mine):
            o_ref[m, :half] = mapped(s_ref[m])
            o_ref[m, half:] = jnp.broadcast_to(
                rows_ref[which, pl.ds(lax.axis_index("local") * mine + m, 1), :], (LANES - half, o_ref.shape[2])
            )


def load_kernel(count, *refs):
    sources, targets, done_ref = refs[:count], refs[count:-1], refs[-1]
    copies = [
        pltpu.make_async_copy(source, target, done_ref.at[i]) for i, (source, target) in enumerate(zip(sources, targets))
    ]
    for copy in copies:
        copy.start()
    for copy in copies:
        copy.wait()


def project_kernel(hd, local, count, *refs):
    pieces = refs[:count]
    weights = refs[count : count + 3]
    grad_ref = refs[count + 3]
    out_refs = refs[count + 4 : -1]
    blocks_ref = refs[-1]
    depth = pieces[0].shape[1]
    rows = pieces[0].shape[0]
    mine = blocks_ref.shape[1]
    sums = []
    for w in weights:
        total = None
        for i, x in enumerate(pieces):
            part = mm(x[...], w[pl.ds(pl.multiple_of(lax.bitwise_xor(lax.axis_index("head"), i) * depth, depth), depth), :])
            total = part if total is None else total + part
        sums.append(total)
    value, key, query = sums
    for h in range(local * mine):
        cols = slice(h * hd, (h + 1) * hd)
        slot = slot_of(lax.axis_index("local"), h // mine, local)
        blocks_ref[slot, h % mine, :rows] = jnp.concatenate([value[:, cols], key[:, cols]], axis=1).astype(BF16)
        blocks_ref[slot, h % mine, rows:] = jnp.concatenate(
            [grad_ref[:, cols].astype(F32), query[:, cols]], axis=1
        ).astype(BF16)
    for s, out_ref in enumerate(out_refs):
        out_ref[...] = blocks_ref[s]


def window_rows(hd, sk):
    tiles = tile_count(sk)
    return (tiles - 1) * hd + hd // (2 * LANES // sk) + 8


def pack_window(total, hd, sk):
    tiles = tile_count(sk)
    used = sk // 2
    short = hd // (LANES // used)
    lane = lane_of(short)
    row = lax.broadcasted_iota(jnp.int32, (8, LANES), 0)
    last = total[:hd, LANES * (tiles - 1) :]
    tail = jnp.zeros((short, LANES), F32)
    for i in range(LANES // used):
        part = last[short * i : short * (i + 1)]
        tail = jnp.where(lane // used == i, pltpu.roll(part, used * i, 1) if i else part, tail)
    sums = jnp.zeros((8, LANES), F32)
    for t in range(tiles):
        sums = jnp.where(row == t, total[hd : hd + 8, LANES * t : LANES * (t + 1)], sums)
    full = [total[:hd, LANES * t : LANES * (t + 1)] for t in range(tiles - 1)]
    return jnp.concatenate(full + [tail, sums], axis=0).astype(BF16)


def unpack_window(packed, hd, sk):
    tiles = tile_count(sk)
    used = sk // 2
    short = hd // (LANES // used)
    lane = lane_of(short)
    end = (tiles - 1) * hd
    rest = packed[end:].astype(F32)
    tail, sums = rest[:short], rest[short:]
    parts = []
    for i in range(LANES // used):
        part = jnp.where(lane < used, pltpu.roll(tail, LANES - used * i, 1) if i else tail, 0.0)
        parts.append(part + pltpu.roll(part, used, 1))
    last = jnp.concatenate(parts, axis=0).astype(BF16)
    state = jnp.concatenate([packed[hd * t : hd * (t + 1)] for t in range(tiles - 1)] + [last], axis=1)
    norm = jnp.concatenate(
        [jnp.broadcast_to(sums[t : t + 1], (16, LANES)) for t in range(tiles)], axis=1
    ).astype(BF16)
    return jnp.concatenate([state, norm], axis=0)


def whole_state(packed, hd, sk):
    both = unpack_window(packed, hd, sk).astype(F32)
    return jnp.concatenate([both[:hd]] + [both[hd:]] * ((LANES - hd) // 16), axis=0)


def key_kernel(sk, hd, local, *refs):
    slots = refs[:local]
    wb_ref, qkv_ref, state_ref, feat_ref, kdot_ref, total_ref = refs[local:]
    blocks, mine, packed, _ = qkv_ref.shape
    for s, slot in enumerate(slots):
        qkv_ref[came_in(lax.axis_index("local"), s, blocks)] = slot[...]
    rows = packed // 2
    width = state_ref.shape[3]
    tiles = width // LANES
    weights = lane_weights(sk, width)
    lane = lane_of(rows)
    for m in range(mine):
        state = jnp.zeros((LANES, width), F32)
        for c in range(blocks):
            state_ref[m, c] = state
            vk = qkv_ref[c, m, :rows]
            e0, e1, d0, d1 = sketched(vk, wb_ref[...])
            e, d = e0 * e1, d0 * d1
            feat = features(e, d, sk, tiles)
            feat_ref[m, c] = feat
            hi, lo = split(e)
            kdot_ref[m, c] = jnp.where(
                lane < 2 * sk, hi.astype(F32), jnp.where(lane < 3 * sk, lo.astype(F32), 0.0)
            ).astype(BF16)
            ones = jnp.where(lane < hd, vk.astype(F32), 1.0).astype(BF16)
            state = state + mm(ones, feat, TN) * weights
        total_ref[m] = pack_window(state, hd, sk)


def query_kernel(
    sk, hd, carry_ref, base_ref, qkv_ref, kdot_ref, state_ref, wb_ref, ba_ref, bb_ref,
    dq_ref, qdot_ref, dn_ref, cot_ref, total_ref,
):
    blocks, mine, packed, _ = qkv_ref.shape
    rows = packed // 2
    half = rows // 2
    width = state_ref.shape[3]
    tiles = width // LANES
    lane = lane_of(rows)
    low = lane < hd
    causal = lax.broadcasted_iota(jnp.int32, (rows, rows), 0) >= lax.broadcasted_iota(
        jnp.int32, (rows, rows), 1
    )
    r_i = lax.broadcasted_iota(jnp.int32, (2 * LANES, LANES), 0) % LANES
    c_i = lax.broadcasted_iota(jnp.int32, (2 * LANES, LANES), 1)
    adder = jnp.where((r_i < hd) & (c_i >= hd), -1.0 / (LANES - hd), 0.0).astype(BF16)
    for m in range(mine):
        total = jnp.zeros((LANES, width), F32)
        base = base_ref[m] if carry_ref is None else base_ref[m] + whole_state(carry_ref[m], hd, sk)
        for c in range(blocks):
            gq = qkv_ref[c, m, rows:]
            e0, e1, d0, d1 = sketched(gq, wb_ref[...])
            e, d = e0 * e1, d0 * d1
            feat = features(e, d, sk, tiles)
            hi, lo = split(e)
            qdot = jnp.where(
                (lane >= sk) & (lane < 2 * sk),
                lo.astype(F32),
                jnp.where(lane < 3 * sk, hi.astype(F32), 0.0),
            ).astype(BF16)
            qdot_ref[m, c] = qdot
            kdot = kdot_ref[m, c]
            state = (base + state_ref[m, c]).astype(BF16)
            ones = jnp.where(low, qkv_ref[c, m, :rows].astype(F32), 1.0).astype(BF16)
            dots = jnp.where(causal, mm(qdot, kdot, NT), 0.0)
            num = mm(feat, state, NT) + mm((dots * dots).astype(BF16), ones)
            inv = 1.0 / (1.0 + num)
            inv = jnp.where(low, pltpu.roll(inv, hd, 1), inv)
            g = gq.astype(F32)
            g_hi, g_lo = split(jnp.where(low, g * num, 0.0))
            den = mm(jnp.concatenate([g_hi, g_lo], axis=1), adder)
            dn = (jnp.where(low, g, den * inv) * inv).astype(BF16)
            dn_ref[m, c] = dn
            cot_dots = (2.0 * dots * mm(dn, ones, NT)).astype(BF16)
            near = mm(cot_dots, kdot)
            cot = mm(dn, state)
            cot_e, cot_d = feature_pull(cot, e, d, sk, tiles)
            cot_e = cot_e + jnp.where((lane < sk) | (lane >= 2 * sk), near, 0.0)
            back = jnp.concatenate(
                [
                    (cot_e * e1).astype(BF16),
                    (cot_e * e0).astype(BF16),
                    (cot_d * d1).astype(BF16),
                    (cot_d * d0).astype(BF16),
                ],
                axis=1,
            )
            dq_ref[m, c] = (mm(back[:half], ba_ref[...]) + mm(back[half:], bb_ref[...])).astype(BF16)
            here = mm(dn, feat, TN)
            cot_ref[m, c] = here
            total = total + here
        total_ref[m] = pack_window(total, hd, sk)


def reverse_kernel(
    sk, hd, others, window_ref, qkv_ref, dq_ref, feat_ref, kdot_ref, qdot_ref, dn_ref, cot_ref, base_ref, wb_ref, bb_ref, *refs
):
    other_refs = refs[:others]
    out_refs = refs[others:-2]
    sum_ref, blocks_ref = refs[-2:]
    window, later = window_ref[...].astype(F32), None
    for d, other_ref in enumerate(other_refs, 1):
        other = other_ref[...].astype(F32)
        window = window + other
        other = jnp.where(lax.axis_index("group") < d, other, 0.0)
        later = other if later is None else later + other
    sum_ref[...] = window.astype(BF16)
    mine, blocks, rows, _ = dn_ref.shape
    packed = rows + rows // 2
    width = base_ref.shape[2]
    tiles = width // LANES
    weights = lane_weights(sk, width)
    lane = lane_of(rows)
    low = lane < hd
    causal = lax.broadcasted_iota(jnp.int32, (rows, rows), 0) <= lax.broadcasted_iota(
        jnp.int32, (rows, rows), 1
    )
    for m in range(mine):
        state = base_ref[m]
        if later is not None:
            state = state + whole_state(later[m].astype(BF16), hd, sk) * weights
        for c in reversed(range(blocks)):
            after = state.astype(BF16)
            vk = qkv_ref[c, m, :rows]
            e0, e1, d0, d1 = sketched(vk, wb_ref[...])
            e, d = e0 * e1, d0 * d1
            qdot = qdot_ref[m, c]
            dn = dn_ref[m, c]
            ones = jnp.where(low, vk.astype(F32), 1.0).astype(BF16)
            dots = jnp.where(causal, mm(kdot_ref[m, c], qdot, NT), 0.0)
            cot_dots = (2.0 * dots * mm(ones, dn, NT)).astype(BF16)
            near = mm(cot_dots, qdot)
            dv = mm(feat_ref[m, c], after, NT) + mm((dots * dots).astype(BF16), dn)
            cot = mm(ones, after)
            cot_e, cot_d = feature_pull(cot, e, d, sk, tiles)
            cot_e = cot_e + jnp.where(lane < 2 * sk, near, 0.0)
            back = jnp.concatenate(
                [
                    (cot_e * e1).astype(BF16),
                    (cot_e * e0).astype(BF16),
                    (cot_d * d1).astype(BF16),
                    (cot_d * d0).astype(BF16),
                ],
                axis=1,
            )
            slot = slot_of(lax.axis_index("local"), c, blocks)
            blocks_ref[slot, m, :rows] = (jnp.where(low, dv, 0.0) + mm(back, bb_ref[...])).astype(BF16)
            blocks_ref[slot, m, rows:] = dq_ref[m, c]
            state = state + cot_ref[m, c] * weights
    for s, out_ref in enumerate(out_refs):
        out_ref[...] = blocks_ref[s]


def input_kernel(hd, local, order, *refs):
    slots = refs[:local]
    weights = refs[local : local + 3]
    dq_ref, dk_ref, dv_ref, out_ref, again_ref, all_ref = refs[local + 3 :]
    _, mine, packed, _ = all_ref.shape
    for s, slot in enumerate(slots):
        all_ref[came_in(lax.axis_index("local"), s, local)] = slot[...]
    rows = packed * 2 // 3
    half = rows // 2
    low = lane_of(rows) < hd

    def block(head):
        return all_ref[head // mine, head % mine].astype(F32)

    for pair in range(local * mine // 2):
        a, b = block(2 * pair), block(2 * pair + 1)
        cols = slice(pair * LANES, (pair + 1) * LANES)
        dv_ref[:, cols] = jnp.where(low, a[:rows], pltpu.roll(b[:rows], hd, 1)).astype(BF16)
        dk_ref[:, cols] = jnp.where(low, pltpu.roll(a[:rows], hd, 1), b[:rows]).astype(BF16)
        a, b = a[rows:], b[rows:]
        dq_ref[:half, cols] = jnp.where(low[:half], a, pltpu.roll(b, hd, 1)).astype(BF16)
        dq_ref[half:, cols] = jnp.where(low[:half], pltpu.roll(a, hd, 1), b).astype(BF16)
    for k, ref in enumerate((dq_ref, dk_ref, dv_ref)):
        again_ref[k] = ref[...]
    head_terms(order, again_ref, weights, out_ref)


def head_terms(order, gradients, weights, out_ref):
    depth = gradients.shape[2]
    dq, dk, dv = (gradients[k] for k in range(3))
    for i in range(out_ref.shape[0]):
        total = None
        for w, x in zip(weights, (dq, dk, dv)):
            part = mm(x, w[pl.ds(pl.multiple_of(lax.bitwise_xor(lax.axis_index("head"), order[i]) * depth, depth), depth), :], NT)
            total = part if total is None else total + part
        out_ref[i] = total.astype(BF16)


def rest_kernel(order, *refs):
    head_terms(order, refs[0], refs[1:4], refs[4])


def expand_kernel(hd, sk, local, *refs):
    slots = refs[:local]
    dstate_ref, dnorm_ref, map_ref, state_ref, norm_ref, all_ref = refs[local:]
    mine = slots[0].shape[0]
    first = slots[0].shape[1] - window_rows(hd, sk)
    heads, rows, width = all_ref.shape
    for s, slot in enumerate(slots):
        for m in range(mine):
            all_ref[came_in(lax.axis_index("local"), s, local) * mine + m] = unpack_window(slot[m, first:], hd, sk)
    spread = mm(all_ref[...].reshape(heads * rows, width), map_ref[...], NT)
    for h in range(heads):
        state_ref[h] = dstate_ref[h] + spread[h * rows : h * rows + hd]
        norm_ref[h : h + 1] = dnorm_ref[h : h + 1] + spread[h * rows + hd : h * rows + hd + 1] * float(LANES - hd)


def call(kernel, name, out_shape, arrays, stay=(), mib=16, scratch=()):
    vmem = pl.BlockSpec(memory_space=pltpu.VMEM)
    return pl.pallas_call(
        kernel,
        in_specs=[vmem] * len(arrays) + [pl.BlockSpec(memory_space=pltpu.HBM)] * len(stay),
        out_specs=[vmem] * len(out_shape),
        out_shape=[jax.ShapeDtypeStruct(dims, kind) for dims, kind in out_shape],
        scratch_shapes=list(scratch),
        compiler_params=pltpu.CompilerParams(vmem_limit_bytes=mib * MIB),
        name=name,
    )(*arrays, *stay)


def hop(x, axis, distance):
    count = lax.axis_size(axis)
    return lax.ppermute(x, axis, [(i, i ^ distance) for i in range(count)])


def body(groups, local, inputs, w_query, w_key, w_value, sketch, prefix_state, prefix_norm, d_attn, d_state_end, d_norm_end):
    rows, depth = inputs.shape
    width = w_query.shape[1]
    heads, feat, hd = prefix_state.shape
    sk = sketch.shape[2]
    tiles = tile_count(sk)
    lanes = tiles * LANES
    half = rows // 2
    packed = rows + half
    mine = heads // local
    ranks = lax.axis_size("head")
    group = lax.axis_index("group")

    def send(x, shift):
        return lax.ppermute(x, "local", [(i, (i + shift) % local) for i in range(local)])

    def exchange(x):
        order = sorted(range(1, local), key=lambda s: -min(s, local - s))
        came = {s: send(x[s], s) for s in order}
        came[0] = x[0]
        return [came[s] for s in range(local)]

    pieces = {0: inputs}
    far = {ranks // 2: hop(inputs, "head", ranks // 2)} if ranks > 1 else {}

    table = jnp.asarray(pair_map(sk), BF16)

    state_t = prefix_state.transpose(0, 2, 1)
    dstate_t = d_state_end.transpose(0, 2, 1)
    loads = (w_value, w_key, w_query, d_attn, inputs)
    loaded = call(
        partial(load_kernel, len(loads)),
        "load",
        [(x.shape, x.dtype) for x in loads],
        [],
        loads,
        mib=8,
        scratch=[pltpu.SemaphoreType.DMA((len(loads),))],
    )
    far, loaded = lax.optimization_barrier((far, list(loaded)))
    pieces.update(far)
    distance = ranks // 4
    while distance:
        pieces.update({at ^ distance: hop(x, "head", distance) for at, x in list(pieces.items())})
        distance //= 2
    keys = list(range(ranks))

    block = ((mine, 2 * rows, LANES), BF16)
    all_blocks = pltpu.VMEM((local,) + block[0], BF16)
    back_blocks = pltpu.VMEM((local, mine, packed, LANES), BF16)
    slots = call(
        partial(project_kernel, hd, local, len(keys)),
        "project",
        [block] * local,
        [loaded[4]] + [pieces[at] for at in keys[1:]] + loaded[:4],
        scratch=[all_blocks],
    )
    sketch, first = lax.optimization_barrier((sketch, slots[0]))
    slots = exchange([first, *slots[1:]])
    base, base_after, wb, ba, bb = call(
        partial(prepare_kernel, sk),
        "prepare",
        [((mine, LANES, lanes), F32)] * 2 + [((4 * hd, 4 * LANES), BF16)] + [((4 * LANES, 2 * hd), BF16)] * 2,
        [sketch.transpose(0, 2, 1), prefix_norm, d_norm_end, table],
        [state_t, dstate_t],
        scratch=[
            pltpu.VMEM((2, heads, lanes), F32),
            pltpu.VMEM((mine, hd, feat), F32),
            pltpu.VMEM((mine, hd, feat), F32),
            pltpu.SemaphoreType.DMA((2,)),
        ],
    )

    small = ((mine, window_rows(hd, sk), LANES), BF16)
    qkv, states, key_feats, kdot, total = call(
        partial(key_kernel, sk, hd, local),
        "key_side",
        [
            ((local, mine, 2 * rows, LANES), BF16),
            ((mine, local, LANES, lanes), F32),
            ((mine, local, rows, lanes), BF16),
            ((mine, local, rows, LANES), BF16),
            small,
        ],
        [*slots, wb],
    )

    carry = []
    for d in range(1, groups):
        carry.append(lax.ppermute(total, "group", [(i, i + d) for i in range(groups - d)]))
    carry = carry[:1] if len(carry) < 2 else [sum(x.astype(F32) for x in carry).astype(BF16)]
    side = partial(query_kernel, sk, hd) if carry else partial(query_kernel, sk, hd, None)
    dq, qdot, dn, cots, window = call(
        side,
        "query_side",
        [
            ((mine, local, half, LANES), BF16),
            ((mine, local, rows, LANES), BF16),
            ((mine, local, rows, LANES), BF16),
            ((mine, local, LANES, lanes), F32),
            small,
        ],
        [*carry, base, qkv, kdot, states, wb, ba, bb],
    )

    others = [lax.ppermute(window, "group", [(i, (i + d) % groups) for i in range(groups)]) for d in range(1, groups)]
    *gradients, window = call(
        partial(reverse_kernel, sk, hd, len(others)),
        "key_gradients",
        [((mine, packed, LANES), BF16)] * local + [small],
        [window, qkv, dq, key_feats, kdot, qdot, dn, cots, base_after, wb, bb, *others],
        scratch=[back_blocks],
    )
    gradients = exchange(gradients)

    window, gradients = lax.optimization_barrier((window, gradients))
    spread = exchange([window] * local)

    order = sorted(range(ranks), key=lambda at: [-(at >> bit & 1) for bit in range(ranks.bit_length() - 1)])
    d_query, d_key, d_value, sums, again = call(
        partial(input_kernel, hd, local, order[: ranks // 2]),
        "input_gradient",
        [((rows, width), BF16)] * 3 + [((ranks // 2, rows, depth), BF16), ((3, rows, width), BF16)],
        [*gradients, w_query, w_key, w_value],
        scratch=[back_blocks],
    )
    came = hop(sums, "head", 1)
    (sums,) = call(
        partial(rest_kernel, order[ranks // 2 :]),
        "input_gradient_rest",
        [((ranks // 2, rows, depth), BF16)],
        [again, w_query, w_key, w_value],
    )
    sums = (sums.astype(F32) + came.astype(F32)).astype(BF16)
    distance = 2
    while distance < ranks:
        count = sums.shape[0] // 2
        came = hop(sums[:count], "head", distance)
        sums = (sums[count:].astype(F32) + came.astype(F32)).astype(BF16)
        distance *= 2

    state_out, d_prefix_norm = call(
        partial(expand_kernel, hd, sk, local),
        "prefix_gradients",
        [((heads, hd, feat), F32), ((heads, feat), F32)],
        [*spread, dstate_t, d_norm_end, table],
        scratch=[pltpu.VMEM((heads, hd + 16, lanes), BF16)],
    )
    d_prefix_state = state_out.transpose(0, 2, 1)
    return sums[0], d_query, d_key, d_value, d_prefix_state, d_prefix_norm


def solution(mesh):
    seq, head = mesh.shape["seq"], mesh.shape["head"]

    def run(*args):
        heads = args[5].shape[0] // head
        local = math.gcd(heads, seq)
        local = min(local & -local, GROUP)
        groups = seq // local
        inner = Mesh(mesh.devices.reshape(groups, local, head), ("group", "local", "head"))
        tokens = ("group", "local")
        return jax.shard_map(
            partial(body, groups, local),
            mesh=inner,
            in_specs=(
                P(tokens, "head"),
                P(None, "head"),
                P(None, "head"),
                P(None, "head"),
                P(),
                P("head", None, None),
                P("head", None),
                P(tokens, "head"),
                P("head", None, None),
                P("head", None),
            ),
            out_specs=(
                P(tokens, "head"),
                P(tokens, "head"),
                P(tokens, "head"),
                P(tokens, "head"),
                P("head", None, None),
                P("head", None),
            ),
            check_vma=False,
        )(*args)

    return run
```

```python
import math
from functools import partial

import jax
import jax.numpy as jnp
import numpy as np
from jax import lax
from jax.experimental import pallas as pl
from jax.experimental.pallas import tpu as pltpu
from jax.sharding import Mesh, PartitionSpec as P

F32 = jnp.float32
BF16 = jnp.bfloat16
LANES = 128
VMEM = pltpu.VMEM
MIB = 1024 * 1024
GROUP = 4

NN = (((1,), (0,)), ((), ()))
NT = (((1,), (1,)), ((), ()))
TN = (((0,), (0,)), ((), ()))


def mm(a, b, dims=NN):
    return lax.dot_general(a, b, dims, preferred_element_type=F32)


def split(x):
    hi = x.astype(BF16)
    return hi, (x - hi.astype(F32)).astype(BF16)


def tile_count(sk):
    return -(-(sk // 2 + 1) // (LANES // sk))


def pair_map(sk):
    step = LANES // sk
    width = tile_count(sk) * LANES
    lane = np.arange(width)
    tile, within = lane // LANES, lane % LANES
    j, a = within // sk, within % sk
    first, second = (a + j) % sk, (a - step * tile) % sk
    keep = step * tile + j <= sk // 2
    table = np.zeros((sk * sk, width), np.float32)
    for one in lane[keep]:
        x, y = first[one], second[one]
        r = step * tile[one] + j[one]
        if r == 0:
            table[x * sk + y, one] = 1.0
        else:
            value = 0.5 if 2 * r == sk else 1.0
            table[x * sk + y, one] = value
            table[y * sk + x, one] = value
    return table


def lane_weights(sk, width):
    lane = lax.broadcasted_iota(jnp.int32, (1, width), 1)
    r = (LANES // sk) * (lane // LANES) + (lane % LANES) // sk
    return jnp.where(
        r <= sk // 2, jnp.where((r == 0) | (2 * r == sk), 1.0, 2.0), 0.0
    ).astype(F32)


def sketched(x, weights):
    both = mm(jnp.concatenate([x, x], axis=1), weights)
    return tuple(both[:, LANES * i : LANES * (i + 1)] for i in range(4))


def turned(e, sk, tiles):
    step = LANES // sk
    return [e] + [pltpu.roll(e, step * t, 1) for t in range(1, tiles)]


def features(e, d, sk, tiles):
    return jnp.concatenate([(d * x).astype(BF16) for x in turned(e, sk, tiles)], axis=1)


def feature_pull(cot, e, d, sk, tiles):
    step = LANES // sk
    cot_e = cot_d = None
    for t, x in enumerate(turned(e, sk, tiles)):
        part = cot[:, LANES * t : LANES * (t + 1)]
        to_d = part * x
        to_e = part * d
        if t:
            to_e = pltpu.roll(to_e, LANES - step * t, 1)
        cot_d = to_d if cot_d is None else cot_d + to_d
        cot_e = to_e if cot_e is None else cot_e + to_e
    return cot_e, cot_d


def lane_of(rows):
    return lax.broadcasted_iota(jnp.int32, (rows, LANES), 1)


def slot_of(place, other, local):
    return lax.rem(other - place + local, local)


def came_in(place, other, local):
    return lax.rem(place - other + local, local)


def prepare_kernel(
    sk, sketch_ref, norm_ref, dnorm_ref, map_ref, states_ref, dstates_ref,
    fwd_ref, bwd_ref, wb_ref, ba_ref, bb_ref, rows_ref, state_ref, dstate_ref, done_ref,
):
    mine, half, _ = state_ref.shape
    own = pl.ds(lax.axis_index("local") * mine, mine)
    copies = [
        pltpu.make_async_copy(states_ref.at[own], state_ref, done_ref.at[0]),
        pltpu.make_async_copy(dstates_ref.at[own], dstate_ref, done_ref.at[1]),
    ]
    for copy in copies:
        copy.start()
    table = map_ref[...]
    step = LANES // sk
    left, right = sketch_ref[0], sketch_ref[1] * sk ** (-0.5)

    def turns(x):
        return [x] + [jnp.concatenate([x[j:], x[:j]], axis=0) for j in range(1, step)]

    full = jnp.concatenate([left] * step + [right] * step + turns(left) + turns(right), axis=0)
    hi, lo = split(full)
    none = jnp.zeros_like(full)
    ba_ref[...] = jnp.concatenate([hi.astype(F32), none], axis=1).astype(BF16)
    bb_ref[...] = jnp.concatenate([none, hi.astype(F32)], axis=1).astype(BF16)
    hi, lo = hi.astype(F32).T, lo.astype(F32).T
    none = jnp.zeros_like(hi)
    wb_ref[...] = jnp.concatenate([none, hi, none, lo], axis=0).astype(BF16)

    def mapped(x):
        hi, lo = split(x)
        return mm(hi, table) + mm(lo, table)

    for which, (s_ref, n_ref, o_ref, scale) in enumerate(
        ((state_ref, norm_ref, fwd_ref, 1.0), (dstate_ref, dnorm_ref, bwd_ref, 1.0 / half))
    ):
        rows_ref[which] = mapped(n_ref[...]) * scale
        copies[which].wait()
        for m in range(mine):
            o_ref[m, :half] = mapped(s_ref[m])
            o_ref[m, half:] = jnp.broadcast_to(
                rows_ref[which, pl.ds(lax.axis_index("local") * mine + m, 1), :], (LANES - half, o_ref.shape[2])
            )


def load_kernel(count, *refs):
    sources, targets, done_ref = refs[:count], refs[count:-1], refs[-1]
    copies = [
        pltpu.make_async_copy(source, target, done_ref.at[i]) for i, (source, target) in enumerate(zip(sources, targets))
    ]
    for copy in copies:
        copy.start()
    for copy in copies:
        copy.wait()


def project_kernel(hd, local, count, *refs):
    pieces = refs[:count]
    weights = refs[count : count + 3]
    grad_ref = refs[count + 3]
    out_refs = refs[count + 4 : -1]
    blocks_ref = refs[-1]
    depth = pieces[0].shape[1]
    rows = pieces[0].shape[0]
    mine = blocks_ref.shape[1]
    sums = []
    for w in weights:
        total = None
        for i, x in enumerate(pieces):
            part = mm(x[...], w[pl.ds(pl.multiple_of(lax.bitwise_xor(lax.axis_index("head"), i) * depth, depth), depth), :])
            total = part if total is None else total + part
        sums.append(total)
    value, key, query = sums
    for h in range(local * mine):
        cols = slice(h * hd, (h + 1) * hd)
        slot = slot_of(lax.axis_index("local"), h // mine, local)
        blocks_ref[slot, h % mine, :rows] = jnp.concatenate([value[:, cols], key[:, cols]], axis=1).astype(BF16)
        blocks_ref[slot, h % mine, rows:] = jnp.concatenate(
            [grad_ref[:, cols].astype(F32), query[:, cols]], axis=1
        ).astype(BF16)
    for s, out_ref in enumerate(out_refs):
        out_ref[...] = blocks_ref[s]


def window_rows(hd, sk):
    tiles = tile_count(sk)
    return (tiles - 1) * hd + hd // (2 * LANES // sk) + 8


def pack_window(total, hd, sk):
    tiles = tile_count(sk)
    used = sk // 2
    short = hd // (LANES // used)
    lane = lane_of(short)
    row = lax.broadcasted_iota(jnp.int32, (8, LANES), 0)
    last = total[:hd, LANES * (tiles - 1) :]
    tail = jnp.zeros((short, LANES), F32)
    for i in range(LANES // used):
        part = last[short * i : short * (i + 1)]
        tail = jnp.where(lane // used == i, pltpu.roll(part, used * i, 1) if i else part, tail)
    sums = jnp.zeros((8, LANES), F32)
    for t in range(tiles):
        sums = jnp.where(row == t, total[hd : hd + 8, LANES * t : LANES * (t + 1)], sums)
    full = [total[:hd, LANES * t : LANES * (t + 1)] for t in range(tiles - 1)]
    return jnp.concatenate(full + [tail, sums], axis=0).astype(BF16)


def unpack_window(packed, hd, sk):
    tiles = tile_count(sk)
    used = sk // 2
    short = hd // (LANES // used)
    lane = lane_of(short)
    end = (tiles - 1) * hd
    rest = packed[end:].astype(F32)
    tail, sums = rest[:short], rest[short:]
    parts = []
    for i in range(LANES // used):
        part = jnp.where(lane < used, pltpu.roll(tail, LANES - used * i, 1) if i else tail, 0.0)
        parts.append(part + pltpu.roll(part, used, 1))
    last = jnp.concatenate(parts, axis=0).astype(BF16)
    state = jnp.concatenate([packed[hd * t : hd * (t + 1)] for t in range(tiles - 1)] + [last], axis=1)
    norm = jnp.concatenate(
        [jnp.broadcast_to(sums[t : t + 1], (16, LANES)) for t in range(tiles)], axis=1
    ).astype(BF16)
    return jnp.concatenate([state, norm], axis=0)


def whole_state(packed, hd, sk):
    both = unpack_window(packed, hd, sk).astype(F32)
    return jnp.concatenate([both[:hd]] + [both[hd:]] * ((LANES - hd) // 16), axis=0)


def key_kernel(sk, hd, local, *refs):
    slots = refs[:local]
    wb_ref, qkv_ref, state_ref, feat_ref, kdot_ref, total_ref = refs[local:]
    blocks, mine, packed, _ = qkv_ref.shape
    for s, slot in enumerate(slots):
        qkv_ref[came_in(lax.axis_index("local"), s, blocks)] = slot[...]
    rows = packed // 2
    width = state_ref.shape[3]
    tiles = width // LANES
    weights = lane_weights(sk, width)
    lane = lane_of(rows)
    for m in range(mine):
        state = jnp.zeros((LANES, width), F32)
        for c in range(blocks):
            state_ref[m, c] = state
            vk = qkv_ref[c, m, :rows]
            e0, e1, d0, d1 = sketched(vk, wb_ref[...])
            e, d = e0 * e1, d0 * d1
            feat = features(e, d, sk, tiles)
            feat_ref[m, c] = feat
            hi, lo = split(e)
            kdot_ref[m, c] = jnp.where(
                lane < 2 * sk, hi.astype(F32), jnp.where(lane < 3 * sk, lo.astype(F32), 0.0)
            ).astype(BF16)
            ones = jnp.where(lane < hd, vk.astype(F32), 1.0).astype(BF16)
            state = state + mm(ones, feat, TN) * weights
        total_ref[m] = pack_window(state, hd, sk)


def query_first_kernel(sk, hd, qkv_ref, kdot_ref, wb_ref, qdot_ref, parts_ref, feat_ref, dots_ref, near_ref):
    blocks, mine, packed, _ = qkv_ref.shape
    rows = packed // 2
    tiles = tile_count(sk)
    lane = lane_of(rows)
    causal = lax.broadcasted_iota(jnp.int32, (rows, rows), 0) >= lax.broadcasted_iota(
        jnp.int32, (rows, rows), 1
    )
    for m in range(mine):
        for c in range(blocks):
            gq = qkv_ref[c, m, rows:]
            e0, e1, d0, d1 = sketched(gq, wb_ref[...])
            e, d = e0 * e1, d0 * d1
            feat = features(e, d, sk, tiles)
            hi, lo = split(e)
            qdot = jnp.where(
                (lane >= sk) & (lane < 2 * sk),
                lo.astype(F32),
                jnp.where(lane < 3 * sk, hi.astype(F32), 0.0),
            ).astype(BF16)
            qdot_ref[m, c] = qdot
            parts_ref[m, c] = jnp.concatenate([e0, e1, d0, d1], axis=1)
            feat_ref[m, c] = feat
            ones = jnp.where(lane < hd, qkv_ref[c, m, :rows].astype(F32), 1.0).astype(BF16)
            dots = jnp.where(causal, mm(qdot, kdot_ref[m, c], NT), 0.0)
            dots_ref[m, c] = dots
            near_ref[m, c] = mm((dots * dots).astype(BF16), ones)


def query_kernel(
    sk, hd, carry_ref, base_ref, qkv_ref, kdot_ref, state_ref, parts_ref, feat_ref, dots_ref, near_ref,
    ba_ref, bb_ref, dq_ref, dn_ref, cot_ref, total_ref,
):
    blocks, mine, packed, _ = qkv_ref.shape
    rows = packed // 2
    half = rows // 2
    width = state_ref.shape[3]
    tiles = width // LANES
    lane = lane_of(rows)
    low = lane < hd
    r_i = lax.broadcasted_iota(jnp.int32, (2 * LANES, LANES), 0) % LANES
    c_i = lax.broadcasted_iota(jnp.int32, (2 * LANES, LANES), 1)
    adder = jnp.where((r_i < hd) & (c_i >= hd), -1.0 / (LANES - hd), 0.0).astype(BF16)
    for m in range(mine):
        total = jnp.zeros((LANES, width), F32)
        base = base_ref[m] if carry_ref is None else base_ref[m] + whole_state(carry_ref[m], hd, sk)
        for c in range(blocks):
            gq = qkv_ref[c, m, rows:]
            e0, e1, d0, d1 = (parts_ref[m, c, :, LANES * i : LANES * (i + 1)] for i in range(4))
            e, d = e0 * e1, d0 * d1
            feat = feat_ref[m, c]
            kdot = kdot_ref[m, c]
            state = (base + state_ref[m, c]).astype(BF16)
            ones = jnp.where(low, qkv_ref[c, m, :rows].astype(F32), 1.0).astype(BF16)
            dots = dots_ref[m, c]
            num = mm(feat, state, NT) + near_ref[m, c]
            inv = 1.0 / (1.0 + num)
            inv = jnp.where(low, pltpu.roll(inv, hd, 1), inv)
            g = gq.astype(F32)
            g_hi, g_lo = split(jnp.where(low, g * num, 0.0))
            den = mm(jnp.concatenate([g_hi, g_lo], axis=1), adder)
            dn = (jnp.where(low, g, den * inv) * inv).astype(BF16)
            dn_ref[m, c] = dn
            cot_dots = (2.0 * dots * mm(dn, ones, NT)).astype(BF16)
            near = mm(cot_dots, kdot)
            cot = mm(dn, state)
            cot_e, cot_d = feature_pull(cot, e, d, sk, tiles)
            cot_e = cot_e + jnp.where((lane < sk) | (lane >= 2 * sk), near, 0.0)
            back = jnp.concatenate(
                [
                    (cot_e * e1).astype(BF16),
                    (cot_e * e0).astype(BF16),
                    (cot_d * d1).astype(BF16),
                    (cot_d * d0).astype(BF16),
                ],
                axis=1,
            )
            dq_ref[m, c] = (mm(back[:half], ba_ref[...]) + mm(back[half:], bb_ref[...])).astype(BF16)
            here = mm(dn, feat, TN)
            cot_ref[m, c] = here
            total = total + here
        total_ref[m] = pack_window(total, hd, sk)


def reverse_first_kernel(sk, hd, qkv_ref, kdot_ref, qdot_ref, dn_ref, wb_ref, parts_ref, near_ref, dv_ref):
    mine, blocks, rows, _ = dn_ref.shape
    lane = lane_of(rows)
    causal = lax.broadcasted_iota(jnp.int32, (rows, rows), 0) <= lax.broadcasted_iota(
        jnp.int32, (rows, rows), 1
    )
    for m in range(mine):
        for c in range(blocks):
            vk = qkv_ref[c, m, :rows]
            parts_ref[m, c] = jnp.concatenate(sketched(vk, wb_ref[...]), axis=1)
            qdot = qdot_ref[m, c]
            dn = dn_ref[m, c]
            ones = jnp.where(lane < hd, vk.astype(F32), 1.0).astype(BF16)
            dots = jnp.where(causal, mm(kdot_ref[m, c], qdot, NT), 0.0)
            cot_dots = (2.0 * dots * mm(ones, dn, NT)).astype(BF16)
            near_ref[m, c] = mm(cot_dots, qdot)
            dv_ref[m, c] = mm((dots * dots).astype(BF16), dn)


def reverse_kernel(
    sk, hd, others, window_ref, qkv_ref, dq_ref, feat_ref, dn_ref, cot_ref, base_ref, parts_ref, near_ref, dv_ref, bb_ref, *refs
):
    other_refs = refs[:others]
    out_refs = refs[others:-2]
    sum_ref, blocks_ref = refs[-2:]
    window, later = window_ref[...].astype(F32), None
    for d, other_ref in enumerate(other_refs, 1):
        other = other_ref[...].astype(F32)
        window = window + other
        other = jnp.where(lax.axis_index("group") < d, other, 0.0)
        later = other if later is None else later + other
    sum_ref[...] = window.astype(BF16)
    mine, blocks, rows, _ = dn_ref.shape
    packed = rows + rows // 2
    width = base_ref.shape[2]
    tiles = width // LANES
    weights = lane_weights(sk, width)
    lane = lane_of(rows)
    low = lane < hd
    for m in range(mine):
        state = base_ref[m]
        if later is not None:
            state = state + whole_state(later[m].astype(BF16), hd, sk) * weights
        for c in reversed(range(blocks)):
            after = state.astype(BF16)
            vk = qkv_ref[c, m, :rows]
            e0, e1, d0, d1 = (parts_ref[m, c, :, LANES * i : LANES * (i + 1)] for i in range(4))
            e, d = e0 * e1, d0 * d1
            ones = jnp.where(low, vk.astype(F32), 1.0).astype(BF16)
            near = near_ref[m, c]
            dv = mm(feat_ref[m, c], after, NT) + dv_ref[m, c]
            cot = mm(ones, after)
            cot_e, cot_d = feature_pull(cot, e, d, sk, tiles)
            cot_e = cot_e + jnp.where(lane < 2 * sk, near, 0.0)
            back = jnp.concatenate(
                [
                    (cot_e * e1).astype(BF16),
                    (cot_e * e0).astype(BF16),
                    (cot_d * d1).astype(BF16),
                    (cot_d * d0).astype(BF16),
                ],
                axis=1,
            )
            slot = slot_of(lax.axis_index("local"), c, blocks)
            blocks_ref[slot, m, :rows] = (jnp.where(low, dv, 0.0) + mm(back, bb_ref[...])).astype(BF16)
            blocks_ref[slot, m, rows:] = dq_ref[m, c]
            state = state + cot_ref[m, c] * weights
    for s, out_ref in enumerate(out_refs):
        out_ref[...] = blocks_ref[s]


def input_kernel(hd, local, order, *refs):
    slots = refs[:local]
    weights = refs[local : local + 3]
    dq_ref, dk_ref, dv_ref, out_ref, again_ref, all_ref = refs[local + 3 :]
    _, mine, packed, _ = all_ref.shape
    for s, slot in enumerate(slots):
        all_ref[came_in(lax.axis_index("local"), s, local)] = slot[...]
    rows = packed * 2 // 3
    half = rows // 2
    low = lane_of(rows) < hd

    def block(head):
        return all_ref[head // mine, head % mine].astype(F32)

    for pair in range(local * mine // 2):
        a, b = block(2 * pair), block(2 * pair + 1)
        cols = slice(pair * LANES, (pair + 1) * LANES)
        dv_ref[:, cols] = jnp.where(low, a[:rows], pltpu.roll(b[:rows], hd, 1)).astype(BF16)
        dk_ref[:, cols] = jnp.where(low, pltpu.roll(a[:rows], hd, 1), b[:rows]).astype(BF16)
        a, b = a[rows:], b[rows:]
        dq_ref[:half, cols] = jnp.where(low[:half], a, pltpu.roll(b, hd, 1)).astype(BF16)
        dq_ref[half:, cols] = jnp.where(low[:half], pltpu.roll(a, hd, 1), b).astype(BF16)
    for k, ref in enumerate((dq_ref, dk_ref, dv_ref)):
        again_ref[k] = ref[...]
    head_terms(order, again_ref, weights, out_ref)


def head_terms(order, gradients, weights, out_ref):
    depth = gradients.shape[2]
    dq, dk, dv = (gradients[k] for k in range(3))
    for i in range(out_ref.shape[0]):
        total = None
        for w, x in zip(weights, (dq, dk, dv)):
            part = mm(x, w[pl.ds(pl.multiple_of(lax.bitwise_xor(lax.axis_index("head"), order[i]) * depth, depth), depth), :], NT)
            total = part if total is None else total + part
        out_ref[i] = total.astype(BF16)


def rest_kernel(order, *refs):
    head_terms(order, refs[0], refs[1:4], refs[4])


def expand_kernel(hd, sk, local, *refs):
    slots = refs[:local]
    dstate_ref, dnorm_ref, map_ref, state_ref, norm_ref, all_ref = refs[local:]
    mine = slots[0].shape[0]
    first = slots[0].shape[1] - window_rows(hd, sk)
    heads, rows, width = all_ref.shape
    for s, slot in enumerate(slots):
        for m in range(mine):
            all_ref[came_in(lax.axis_index("local"), s, local) * mine + m] = unpack_window(slot[m, first:], hd, sk)
    spread = mm(all_ref[...].reshape(heads * rows, width), map_ref[...], NT)
    for h in range(heads):
        state_ref[h] = dstate_ref[h] + spread[h * rows : h * rows + hd]
        norm_ref[h : h + 1] = dnorm_ref[h : h + 1] + spread[h * rows + hd : h * rows + hd + 1] * float(LANES - hd)


def call(kernel, name, out_shape, arrays, stay=(), mib=16, scratch=()):
    vmem = pl.BlockSpec(memory_space=pltpu.VMEM)
    return pl.pallas_call(
        kernel,
        in_specs=[vmem] * len(arrays) + [pl.BlockSpec(memory_space=pltpu.HBM)] * len(stay),
        out_specs=[vmem] * len(out_shape),
        out_shape=[jax.ShapeDtypeStruct(dims, kind) for dims, kind in out_shape],
        scratch_shapes=list(scratch),
        compiler_params=pltpu.CompilerParams(vmem_limit_bytes=mib * MIB),
        name=name,
    )(*arrays, *stay)


def hop(x, axis, distance):
    count = lax.axis_size(axis)
    return lax.ppermute(x, axis, [(i, i ^ distance) for i in range(count)])


def body(groups, local, inputs, w_query, w_key, w_value, sketch, prefix_state, prefix_norm, d_attn, d_state_end, d_norm_end):
    rows, depth = inputs.shape
    width = w_query.shape[1]
    heads, feat, hd = prefix_state.shape
    sk = sketch.shape[2]
    tiles = tile_count(sk)
    lanes = tiles * LANES
    half = rows // 2
    packed = rows + half
    mine = heads // local
    ranks = lax.axis_size("head")
    group = lax.axis_index("group")

    def send(x, shift):
        return lax.ppermute(x, "local", [(i, (i + shift) % local) for i in range(local)])

    def exchange(x):
        order = sorted(range(1, local), key=lambda s: -min(s, local - s))
        came = {s: send(x[s], s) for s in order}
        came[0] = x[0]
        return [came[s] for s in range(local)]

    pieces = {0: inputs}
    far = {ranks // 2: hop(inputs, "head", ranks // 2)} if ranks > 1 else {}

    table = jnp.asarray(pair_map(sk), BF16)

    state_t = prefix_state.transpose(0, 2, 1)
    dstate_t = d_state_end.transpose(0, 2, 1)
    loads = (w_value, w_key, w_query, d_attn, inputs)
    loaded = call(
        partial(load_kernel, len(loads)),
        "load",
        [(x.shape, x.dtype) for x in loads],
        [],
        loads,
        mib=8,
        scratch=[pltpu.SemaphoreType.DMA((len(loads),))],
    )
    far, loaded = lax.optimization_barrier((far, list(loaded)))
    pieces.update(far)
    distance = ranks // 4
    while distance:
        pieces.update({at ^ distance: hop(x, "head", distance) for at, x in list(pieces.items())})
        distance //= 2
    keys = list(range(ranks))

    block = ((mine, 2 * rows, LANES), BF16)
    all_blocks = pltpu.VMEM((local,) + block[0], BF16)
    back_blocks = pltpu.VMEM((local, mine, packed, LANES), BF16)
    slots = call(
        partial(project_kernel, hd, local, len(keys)),
        "project",
        [block] * local,
        [loaded[4]] + [pieces[at] for at in keys[1:]] + loaded[:4],
        scratch=[all_blocks],
    )
    sketch, first = lax.optimization_barrier((sketch, slots[0]))
    slots = exchange([first, *slots[1:]])
    base, base_after, wb, ba, bb = call(
        partial(prepare_kernel, sk),
        "prepare",
        [((mine, LANES, lanes), F32)] * 2 + [((4 * hd, 4 * LANES), BF16)] + [((4 * LANES, 2 * hd), BF16)] * 2,
        [sketch.transpose(0, 2, 1), prefix_norm, d_norm_end, table],
        [state_t, dstate_t],
        scratch=[
            pltpu.VMEM((2, heads, lanes), F32),
            pltpu.VMEM((mine, hd, feat), F32),
            pltpu.VMEM((mine, hd, feat), F32),
            pltpu.SemaphoreType.DMA((2,)),
        ],
    )

    small = ((mine, window_rows(hd, sk), LANES), BF16)
    qkv, states, key_feats, kdot, total = call(
        partial(key_kernel, sk, hd, local),
        "key_side",
        [
            ((local, mine, 2 * rows, LANES), BF16),
            ((mine, local, LANES, lanes), F32),
            ((mine, local, rows, lanes), BF16),
            ((mine, local, rows, LANES), BF16),
            small,
        ],
        [*slots, wb],
    )

    carry = []
    for d in range(1, groups):
        carry.append(lax.ppermute(total, "group", [(i, i + d) for i in range(groups - d)]))
    carry = carry[:1] if len(carry) < 2 else [sum(x.astype(F32) for x in carry).astype(BF16)]
    side = partial(query_kernel, sk, hd) if carry else partial(query_kernel, sk, hd, None)
    whole = ((mine, local, rows, LANES), F32)
    parts = ((mine, local, rows, 4 * LANES), F32)
    qdot, query_parts, query_feats, dots, near = call(
        partial(query_first_kernel, sk, hd),
        "query_first",
        [
            ((mine, local, rows, LANES), BF16),
            parts,
            ((mine, local, rows, lanes), BF16),
            ((mine, local, rows, rows), F32),
            whole,
        ],
        [qkv, kdot, wb],
    )
    dq, dn, cots, window = call(
        side,
        "query_side",
        [
            ((mine, local, half, LANES), BF16),
            ((mine, local, rows, LANES), BF16),
            ((mine, local, LANES, lanes), F32),
            small,
        ],
        [*carry, base, qkv, kdot, states, query_parts, query_feats, dots, near, ba, bb],
    )

    others = [lax.ppermute(window, "group", [(i, (i + d) % groups) for i in range(groups)]) for d in range(1, groups)]
    key_parts, key_near, dv = call(
        partial(reverse_first_kernel, sk, hd),
        "key_first",
        [parts, whole, whole],
        [qkv, kdot, qdot, dn, wb],
    )
    *gradients, window = call(
        partial(reverse_kernel, sk, hd, len(others)),
        "key_gradients",
        [((mine, packed, LANES), BF16)] * local + [small],
        [window, qkv, dq, key_feats, dn, cots, base_after, key_parts, key_near, dv, bb, *others],
        scratch=[back_blocks],
    )
    gradients = exchange(gradients)

    window, gradients = lax.optimization_barrier((window, gradients))
    spread = exchange([window] * local)

    order = sorted(range(ranks), key=lambda at: [-(at >> bit & 1) for bit in range(ranks.bit_length() - 1)])
    d_query, d_key, d_value, sums, again = call(
        partial(input_kernel, hd, local, order[: ranks // 2]),
        "input_gradient",
        [((rows, width), BF16)] * 3 + [((ranks // 2, rows, depth), BF16), ((3, rows, width), BF16)],
        [*gradients, w_query, w_key, w_value],
        scratch=[back_blocks],
    )
    came = hop(sums, "head", 1)
    (sums,) = call(
        partial(rest_kernel, order[ranks // 2 :]),
        "input_gradient_rest",
        [((ranks // 2, rows, depth), BF16)],
        [again, w_query, w_key, w_value],
    )
    sums = (sums.astype(F32) + came.astype(F32)).astype(BF16)
    distance = 2
    while distance < ranks:
        count = sums.shape[0] // 2
        came = hop(sums[:count], "head", distance)
        sums = (sums[count:].astype(F32) + came.astype(F32)).astype(BF16)
        distance *= 2

    state_out, d_prefix_norm = call(
        partial(expand_kernel, hd, sk, local),
        "prefix_gradients",
        [((heads, hd, feat), F32), ((heads, feat), F32)],
        [*spread, dstate_t, d_norm_end, table],
        scratch=[pltpu.VMEM((heads, hd + 16, lanes), BF16)],
    )
    d_prefix_state = state_out.transpose(0, 2, 1)
    return sums[0], d_query, d_key, d_value, d_prefix_state, d_prefix_norm


def solution(mesh):
    seq, head = mesh.shape["seq"], mesh.shape["head"]

    def run(*args):
        heads = args[5].shape[0] // head
        local = math.gcd(heads, seq)
        local = min(local & -local, GROUP)
        groups = seq // local
        inner = Mesh(mesh.devices.reshape(groups, local, head), ("group", "local", "head"))
        tokens = ("group", "local")
        return jax.shard_map(
            partial(body, groups, local),
            mesh=inner,
            in_specs=(
                P(tokens, "head"),
                P(None, "head"),
                P(None, "head"),
                P(None, "head"),
                P(),
                P("head", None, None),
                P("head", None),
                P(tokens, "head"),
                P("head", None, None),
                P("head", None),
            ),
            out_specs=(
                P(tokens, "head"),
                P(tokens, "head"),
                P(tokens, "head"),
                P(tokens, "head"),
                P("head", None, None),
                P("head", None),
            ),
            check_vma=False,
        )(*args)

    return run
```

```python
import math
from functools import partial

import jax
import jax.numpy as jnp
import numpy as np
from jax import lax
from jax.experimental import pallas as pl
from jax.experimental.pallas import tpu as pltpu
from jax.sharding import Mesh, PartitionSpec as P

F32 = jnp.float32
BF16 = jnp.bfloat16
LANES = 128
VMEM = pltpu.VMEM
MIB = 1024 * 1024
GROUP = 4

NN = (((1,), (0,)), ((), ()))
NT = (((1,), (1,)), ((), ()))
TN = (((0,), (0,)), ((), ()))


def mm(a, b, dims=NN):
    return lax.dot_general(a, b, dims, preferred_element_type=F32)


def split(x):
    hi = x.astype(BF16)
    return hi, (x - hi.astype(F32)).astype(BF16)


def tile_count(sk):
    return -(-(sk // 2 + 1) // (LANES // sk))


def pair_map(sk):
    step = LANES // sk
    width = tile_count(sk) * LANES
    lane = np.arange(width)
    tile, within = lane // LANES, lane % LANES
    j, a = within // sk, within % sk
    first, second = (a + j) % sk, (a - step * tile) % sk
    keep = step * tile + j <= sk // 2
    table = np.zeros((sk * sk, width), np.float32)
    for one in lane[keep]:
        x, y = first[one], second[one]
        r = step * tile[one] + j[one]
        if r == 0:
            table[x * sk + y, one] = 1.0
        else:
            value = 0.5 if 2 * r == sk else 1.0
            table[x * sk + y, one] = value
            table[y * sk + x, one] = value
    return table


def lane_weights(sk, width):
    lane = lax.broadcasted_iota(jnp.int32, (1, width), 1)
    r = (LANES // sk) * (lane // LANES) + (lane % LANES) // sk
    return jnp.where(
        r <= sk // 2, jnp.where((r == 0) | (2 * r == sk), 1.0, 2.0), 0.0
    ).astype(F32)


def sketched(x, weights):
    both = mm(jnp.concatenate([x, x], axis=1), weights)
    return tuple(both[:, LANES * i : LANES * (i + 1)] for i in range(4))


def turned(e, sk, tiles):
    step = LANES // sk
    return [e] + [pltpu.roll(e, step * t, 1) for t in range(1, tiles)]


def features(e, d, sk, tiles):
    return jnp.concatenate([(d * x).astype(BF16) for x in turned(e, sk, tiles)], axis=1)


def feature_pull(cot, e, d, sk, tiles):
    step = LANES // sk
    cot_e = cot_d = None
    for t, x in enumerate(turned(e, sk, tiles)):
        part = cot[:, LANES * t : LANES * (t + 1)]
        to_d = part * x
        to_e = part * d
        if t:
            to_e = pltpu.roll(to_e, LANES - step * t, 1)
        cot_d = to_d if cot_d is None else cot_d + to_d
        cot_e = to_e if cot_e is None else cot_e + to_e
    return cot_e, cot_d


def lane_of(rows):
    return lax.broadcasted_iota(jnp.int32, (rows, LANES), 1)


def slot_of(place, other, local):
    return lax.bitwise_xor(place, other)


def came_in(place, other, local):
    return lax.bitwise_xor(place, other)


def prepare_kernel(
    sk, sketch_ref, norm_ref, dnorm_ref, map_ref, states_ref, dstates_ref,
    fwd_ref, bwd_ref, wb_ref, ba_ref, bb_ref, rows_ref, state_ref, dstate_ref, done_ref,
):
    mine, half, _ = state_ref.shape
    own = pl.ds(lax.axis_index("local") * mine, mine)
    copies = [
        pltpu.make_async_copy(states_ref.at[own], state_ref, done_ref.at[0]),
        pltpu.make_async_copy(dstates_ref.at[own], dstate_ref, done_ref.at[1]),
    ]
    for copy in copies:
        copy.start()
    table = map_ref[...]
    step = LANES // sk
    left, right = sketch_ref[0], sketch_ref[1] * sk ** (-0.5)

    def turns(x):
        return [x] + [jnp.concatenate([x[j:], x[:j]], axis=0) for j in range(1, step)]

    full = jnp.concatenate([left] * step + [right] * step + turns(left) + turns(right), axis=0)
    hi, lo = split(full)
    none = jnp.zeros_like(full)
    ba_ref[...] = jnp.concatenate([hi.astype(F32), none], axis=1).astype(BF16)
    bb_ref[...] = jnp.concatenate([none, hi.astype(F32)], axis=1).astype(BF16)
    hi, lo = hi.astype(F32).T, lo.astype(F32).T
    none = jnp.zeros_like(hi)
    wb_ref[...] = jnp.concatenate([none, hi, none, lo], axis=0).astype(BF16)

    def mapped(x):
        hi, lo = split(x)
        return mm(hi, table) + mm(lo, table)

    for which, (s_ref, n_ref, o_ref, scale) in enumerate(
        ((state_ref, norm_ref, fwd_ref, 1.0), (dstate_ref, dnorm_ref, bwd_ref, 1.0 / half))
    ):
        rows_ref[which] = mapped(n_ref[...]) * scale
        copies[which].wait()
        for m in range(mine):
            o_ref[m, :half] = mapped(s_ref[m])
            o_ref[m, half:] = jnp.broadcast_to(
                rows_ref[which, pl.ds(lax.axis_index("local") * mine + m, 1), :], (LANES - half, o_ref.shape[2])
            )


def load_kernel(count, *refs):
    sources, targets, done_ref = refs[:count], refs[count:-1], refs[-1]
    copies = [
        pltpu.make_async_copy(source, target, done_ref.at[i]) for i, (source, target) in enumerate(zip(sources, targets))
    ]
    for copy in copies:
        copy.start()
    for copy in copies:
        copy.wait()


def project_kernel(hd, local, count, *refs):
    pieces = refs[:count]
    weights = refs[count : count + 3]
    grad_ref = refs[count + 3]
    out_refs = refs[count + 4 : -1]
    blocks_ref = refs[-1]
    depth = pieces[0].shape[1]
    rows = pieces[0].shape[0]
    mine = blocks_ref.shape[1]
    sums = []
    for w in weights:
        total = None
        for i, x in enumerate(pieces):
            part = mm(x[...], w[pl.ds(pl.multiple_of(lax.bitwise_xor(lax.axis_index("head"), i) * depth, depth), depth), :])
            total = part if total is None else total + part
        sums.append(total)
    value, key, query = sums
    for h in range(local * mine):
        cols = slice(h * hd, (h + 1) * hd)
        slot = slot_of(lax.axis_index("local"), h // mine, local)
        blocks_ref[slot, h % mine, :rows] = jnp.concatenate([value[:, cols], key[:, cols]], axis=1).astype(BF16)
        blocks_ref[slot, h % mine, rows:] = jnp.concatenate(
            [grad_ref[:, cols].astype(F32), query[:, cols]], axis=1
        ).astype(BF16)
    for s, out_ref in enumerate(out_refs):
        out_ref[...] = blocks_ref[s]


def window_rows(hd, sk):
    tiles = tile_count(sk)
    return (tiles - 1) * hd + hd // (2 * LANES // sk) + 8


def pack_window(total, hd, sk):
    tiles = tile_count(sk)
    used = sk // 2
    short = hd // (LANES // used)
    lane = lane_of(short)
    row = lax.broadcasted_iota(jnp.int32, (8, LANES), 0)
    last = total[:hd, LANES * (tiles - 1) :]
    tail = jnp.zeros((short, LANES), F32)
    for i in range(LANES // used):
        part = last[short * i : short * (i + 1)]
        tail = jnp.where(lane // used == i, pltpu.roll(part, used * i, 1) if i else part, tail)
    sums = jnp.zeros((8, LANES), F32)
    for t in range(tiles):
        sums = jnp.where(row == t, total[hd : hd + 8, LANES * t : LANES * (t + 1)], sums)
    full = [total[:hd, LANES * t : LANES * (t + 1)] for t in range(tiles - 1)]
    return jnp.concatenate(full + [tail, sums], axis=0).astype(BF16)


def unpack_window(packed, hd, sk):
    tiles = tile_count(sk)
    used = sk // 2
    short = hd // (LANES // used)
    lane = lane_of(short)
    end = (tiles - 1) * hd
    rest = packed[end:].astype(F32)
    tail, sums = rest[:short], rest[short:]
    parts = []
    for i in range(LANES // used):
        part = jnp.where(lane < used, pltpu.roll(tail, LANES - used * i, 1) if i else tail, 0.0)
        parts.append(part + pltpu.roll(part, used, 1))
    last = jnp.concatenate(parts, axis=0).astype(BF16)
    state = jnp.concatenate([packed[hd * t : hd * (t + 1)] for t in range(tiles - 1)] + [last], axis=1)
    norm = jnp.concatenate(
        [jnp.broadcast_to(sums[t : t + 1], (16, LANES)) for t in range(tiles)], axis=1
    ).astype(BF16)
    return jnp.concatenate([state, norm], axis=0)


def whole_state(packed, hd, sk):
    both = unpack_window(packed, hd, sk).astype(F32)
    return jnp.concatenate([both[:hd]] + [both[hd:]] * ((LANES - hd) // 16), axis=0)


def key_kernel(sk, hd, local, *refs):
    slots = refs[:local]
    wb_ref, qkv_ref, state_ref, feat_ref, kdot_ref, total_ref = refs[local:]
    blocks, mine, packed, _ = qkv_ref.shape
    for s, slot in enumerate(slots):
        qkv_ref[came_in(lax.axis_index("local"), s, blocks)] = slot[...]
    rows = packed // 2
    width = state_ref.shape[3]
    tiles = width // LANES
    weights = lane_weights(sk, width)
    lane = lane_of(rows)
    for m in range(mine):
        state = jnp.zeros((LANES, width), F32)
        for c in range(blocks):
            state_ref[m, c] = state
            vk = qkv_ref[c, m, :rows]
            e0, e1, d0, d1 = sketched(vk, wb_ref[...])
            e, d = e0 * e1, d0 * d1
            feat = features(e, d, sk, tiles)
            feat_ref[m, c] = feat
            hi, lo = split(e)
            kdot_ref[m, c] = jnp.where(
                lane < 2 * sk, hi.astype(F32), jnp.where(lane < 3 * sk, lo.astype(F32), 0.0)
            ).astype(BF16)
            ones = jnp.where(lane < hd, vk.astype(F32), 1.0).astype(BF16)
            state = state + mm(ones, feat, TN) * weights
        total_ref[m] = pack_window(state, hd, sk)


def query_first_kernel(sk, hd, qkv_ref, kdot_ref, wb_ref, qdot_ref, parts_ref, feat_ref, dots_ref, near_ref):
    blocks, mine, packed, _ = qkv_ref.shape
    rows = packed // 2
    tiles = tile_count(sk)
    lane = lane_of(rows)
    causal = lax.broadcasted_iota(jnp.int32, (rows, rows), 0) >= lax.broadcasted_iota(
        jnp.int32, (rows, rows), 1
    )
    for m in range(mine):
        for c in range(blocks):
            gq = qkv_ref[c, m, rows:]
            e0, e1, d0, d1 = sketched(gq, wb_ref[...])
            e, d = e0 * e1, d0 * d1
            feat = features(e, d, sk, tiles)
            hi, lo = split(e)
            qdot = jnp.where(
                (lane >= sk) & (lane < 2 * sk),
                lo.astype(F32),
                jnp.where(lane < 3 * sk, hi.astype(F32), 0.0),
            ).astype(BF16)
            qdot_ref[m, c] = qdot
            parts_ref[m, c] = jnp.concatenate([e0, e1, d0, d1], axis=1)
            feat_ref[m, c] = feat
            ones = jnp.where(lane < hd, qkv_ref[c, m, :rows].astype(F32), 1.0).astype(BF16)
            dots = jnp.where(causal, mm(qdot, kdot_ref[m, c], NT), 0.0)
            dots_ref[m, c] = dots
            near_ref[m, c] = mm((dots * dots).astype(BF16), ones)


def query_kernel(
    sk, hd, carry_ref, base_ref, qkv_ref, kdot_ref, state_ref, parts_ref, feat_ref, dots_ref, near_ref,
    ba_ref, bb_ref, dq_ref, dn_ref, cot_ref, total_ref,
):
    blocks, mine, packed, _ = qkv_ref.shape
    rows = packed // 2
    half = rows // 2
    width = state_ref.shape[3]
    tiles = width // LANES
    lane = lane_of(rows)
    low = lane < hd
    r_i = lax.broadcasted_iota(jnp.int32, (2 * LANES, LANES), 0) % LANES
    c_i = lax.broadcasted_iota(jnp.int32, (2 * LANES, LANES), 1)
    adder = jnp.where((r_i < hd) & (c_i >= hd), -1.0 / (LANES - hd), 0.0).astype(BF16)
    for m in range(mine):
        total = jnp.zeros((LANES, width), F32)
        base = base_ref[m] if carry_ref is None else base_ref[m] + whole_state(carry_ref[m], hd, sk)
        for c in range(blocks):
            gq = qkv_ref[c, m, rows:]
            e0, e1, d0, d1 = (parts_ref[m, c, :, LANES * i : LANES * (i + 1)] for i in range(4))
            e, d = e0 * e1, d0 * d1
            feat = feat_ref[m, c]
            kdot = kdot_ref[m, c]
            state = (base + state_ref[m, c]).astype(BF16)
            ones = jnp.where(low, qkv_ref[c, m, :rows].astype(F32), 1.0).astype(BF16)
            dots = dots_ref[m, c]
            num = mm(feat, state, NT) + near_ref[m, c]
            inv = 1.0 / (1.0 + num)
            inv = jnp.where(low, pltpu.roll(inv, hd, 1), inv)
            g = gq.astype(F32)
            g_hi, g_lo = split(jnp.where(low, g * num, 0.0))
            den = mm(jnp.concatenate([g_hi, g_lo], axis=1), adder)
            dn = (jnp.where(low, g, den * inv) * inv).astype(BF16)
            dn_ref[m, c] = dn
            cot_dots = (2.0 * dots * mm(dn, ones, NT)).astype(BF16)
            near = mm(cot_dots, kdot)
            cot = mm(dn, state)
            cot_e, cot_d = feature_pull(cot, e, d, sk, tiles)
            cot_e = cot_e + jnp.where((lane < sk) | (lane >= 2 * sk), near, 0.0)
            back = jnp.concatenate(
                [
                    (cot_e * e1).astype(BF16),
                    (cot_e * e0).astype(BF16),
                    (cot_d * d1).astype(BF16),
                    (cot_d * d0).astype(BF16),
                ],
                axis=1,
            )
            dq_ref[m, c] = (mm(back[:half], ba_ref[...]) + mm(back[half:], bb_ref[...])).astype(BF16)
            here = mm(dn, feat, TN)
            cot_ref[m, c] = here
            total = total + here
        total_ref[m] = pack_window(total, hd, sk)


def reverse_first_kernel(sk, hd, qkv_ref, kdot_ref, qdot_ref, dn_ref, wb_ref, parts_ref, near_ref, dv_ref):
    mine, blocks, rows, _ = dn_ref.shape
    lane = lane_of(rows)
    causal = lax.broadcasted_iota(jnp.int32, (rows, rows), 0) <= lax.broadcasted_iota(
        jnp.int32, (rows, rows), 1
    )
    for m in range(mine):
        for c in range(blocks):
            vk = qkv_ref[c, m, :rows]
            parts_ref[m, c] = jnp.concatenate(sketched(vk, wb_ref[...]), axis=1)
            qdot = qdot_ref[m, c]
            dn = dn_ref[m, c]
            ones = jnp.where(lane < hd, vk.astype(F32), 1.0).astype(BF16)
            dots = jnp.where(causal, mm(kdot_ref[m, c], qdot, NT), 0.0)
            cot_dots = (2.0 * dots * mm(ones, dn, NT)).astype(BF16)
            near_ref[m, c] = mm(cot_dots, qdot)
            dv_ref[m, c] = mm((dots * dots).astype(BF16), dn)


def reverse_kernel(
    sk, hd, others, window_ref, qkv_ref, dq_ref, feat_ref, dn_ref, cot_ref, base_ref, parts_ref, near_ref, dv_ref, bb_ref, *refs
):
    other_refs = refs[:others]
    out_refs = refs[others:-2]
    sum_ref, blocks_ref = refs[-2:]
    window, later = window_ref[...].astype(F32), None
    for d, other_ref in enumerate(other_refs, 1):
        other = other_ref[...].astype(F32)
        window = window + other
        other = jnp.where(lax.axis_index("group") < d, other, 0.0)
        later = other if later is None else later + other
    sum_ref[...] = window.astype(BF16)
    mine, blocks, rows, _ = dn_ref.shape
    packed = rows + rows // 2
    width = base_ref.shape[2]
    tiles = width // LANES
    weights = lane_weights(sk, width)
    lane = lane_of(rows)
    low = lane < hd
    for m in range(mine):
        state = base_ref[m]
        if later is not None:
            state = state + whole_state(later[m].astype(BF16), hd, sk) * weights
        for c in reversed(range(blocks)):
            after = state.astype(BF16)
            vk = qkv_ref[c, m, :rows]
            e0, e1, d0, d1 = (parts_ref[m, c, :, LANES * i : LANES * (i + 1)] for i in range(4))
            e, d = e0 * e1, d0 * d1
            ones = jnp.where(low, vk.astype(F32), 1.0).astype(BF16)
            near = near_ref[m, c]
            dv = mm(feat_ref[m, c], after, NT) + dv_ref[m, c]
            cot = mm(ones, after)
            cot_e, cot_d = feature_pull(cot, e, d, sk, tiles)
            cot_e = cot_e + jnp.where(lane < 2 * sk, near, 0.0)
            back = jnp.concatenate(
                [
                    (cot_e * e1).astype(BF16),
                    (cot_e * e0).astype(BF16),
                    (cot_d * d1).astype(BF16),
                    (cot_d * d0).astype(BF16),
                ],
                axis=1,
            )
            slot = slot_of(lax.axis_index("local"), c, blocks)
            blocks_ref[slot, m, :rows] = (jnp.where(low, dv, 0.0) + mm(back, bb_ref[...])).astype(BF16)
            blocks_ref[slot, m, rows:] = dq_ref[m, c]
            state = state + cot_ref[m, c] * weights
    for s, out_ref in enumerate(out_refs):
        out_ref[...] = blocks_ref[s]


def input_kernel(hd, local, order, *refs):
    slots = refs[:local]
    weights = refs[local : local + 3]
    dq_ref, dk_ref, dv_ref, out_ref, again_ref, all_ref = refs[local + 3 :]
    _, mine, packed, _ = all_ref.shape
    for s, slot in enumerate(slots):
        all_ref[came_in(lax.axis_index("local"), s, local)] = slot[...]
    rows = packed * 2 // 3
    half = rows // 2
    low = lane_of(rows) < hd

    def block(head):
        return all_ref[head // mine, head % mine].astype(F32)

    for pair in range(local * mine // 2):
        a, b = block(2 * pair), block(2 * pair + 1)
        cols = slice(pair * LANES, (pair + 1) * LANES)
        dv_ref[:, cols] = jnp.where(low, a[:rows], pltpu.roll(b[:rows], hd, 1)).astype(BF16)
        dk_ref[:, cols] = jnp.where(low, pltpu.roll(a[:rows], hd, 1), b[:rows]).astype(BF16)
        a, b = a[rows:], b[rows:]
        dq_ref[:half, cols] = jnp.where(low[:half], a, pltpu.roll(b, hd, 1)).astype(BF16)
        dq_ref[half:, cols] = jnp.where(low[:half], pltpu.roll(a, hd, 1), b).astype(BF16)
    for k, ref in enumerate((dq_ref, dk_ref, dv_ref)):
        again_ref[k] = ref[...]
    head_terms(order, again_ref, weights, out_ref)


def head_terms(order, gradients, weights, out_ref):
    depth = gradients.shape[2]
    dq, dk, dv = (gradients[k] for k in range(3))
    for i in range(out_ref.shape[0]):
        total = None
        for w, x in zip(weights, (dq, dk, dv)):
            part = mm(x, w[pl.ds(pl.multiple_of(lax.bitwise_xor(lax.axis_index("head"), order[i]) * depth, depth), depth), :], NT)
            total = part if total is None else total + part
        out_ref[i] = total.astype(BF16)


def rest_kernel(order, *refs):
    head_terms(order, refs[0], refs[1:4], refs[4])


def expand_kernel(hd, sk, local, *refs):
    slots = refs[:local]
    dstate_ref, dnorm_ref, map_ref, state_ref, norm_ref, all_ref = refs[local:]
    mine = slots[0].shape[0]
    first = slots[0].shape[1] - window_rows(hd, sk)
    heads, rows, width = all_ref.shape
    for s, slot in enumerate(slots):
        for m in range(mine):
            all_ref[came_in(lax.axis_index("local"), s, local) * mine + m] = unpack_window(slot[m, first:], hd, sk)
    spread = mm(all_ref[...].reshape(heads * rows, width), map_ref[...], NT)
    for h in range(heads):
        state_ref[h] = dstate_ref[h] + spread[h * rows : h * rows + hd]
        norm_ref[h : h + 1] = dnorm_ref[h : h + 1] + spread[h * rows + hd : h * rows + hd + 1] * float(LANES - hd)


def call(kernel, name, out_shape, arrays, stay=(), mib=16, scratch=()):
    vmem = pl.BlockSpec(memory_space=pltpu.VMEM)
    return pl.pallas_call(
        kernel,
        in_specs=[vmem] * len(arrays) + [pl.BlockSpec(memory_space=pltpu.HBM)] * len(stay),
        out_specs=[vmem] * len(out_shape),
        out_shape=[jax.ShapeDtypeStruct(dims, kind) for dims, kind in out_shape],
        scratch_shapes=list(scratch),
        compiler_params=pltpu.CompilerParams(vmem_limit_bytes=mib * MIB),
        name=name,
    )(*arrays, *stay)


def hop(x, axis, distance):
    count = lax.axis_size(axis)
    return lax.ppermute(x, axis, [(i, i ^ distance) for i in range(count)])


def body(groups, local, inputs, w_query, w_key, w_value, sketch, prefix_state, prefix_norm, d_attn, d_state_end, d_norm_end):
    rows, depth = inputs.shape
    width = w_query.shape[1]
    heads, feat, hd = prefix_state.shape
    sk = sketch.shape[2]
    tiles = tile_count(sk)
    lanes = tiles * LANES
    half = rows // 2
    packed = rows + half
    mine = heads // local
    ranks = lax.axis_size("head")
    group = lax.axis_index("group")

    def send(x, shift):
        return lax.ppermute(x, "local", [(i, i ^ shift) for i in range(local)])

    def exchange(x):
        order = sorted(range(1, local), key=lambda s: -min(s, local - s))
        came = {s: send(x[s], s) for s in order}
        came[0] = x[0]
        return [came[s] for s in range(local)]

    pieces = {0: inputs}
    far = {ranks // 2: hop(inputs, "head", ranks // 2)} if ranks > 1 else {}

    table = jnp.asarray(pair_map(sk), BF16)

    state_t = prefix_state.transpose(0, 2, 1)
    dstate_t = d_state_end.transpose(0, 2, 1)
    loads = (w_value, w_key, w_query, d_attn, inputs)
    loaded = call(
        partial(load_kernel, len(loads)),
        "load",
        [(x.shape, x.dtype) for x in loads],
        [],
        loads,
        mib=8,
        scratch=[pltpu.SemaphoreType.DMA((len(loads),))],
    )
    far, loaded = lax.optimization_barrier((far, list(loaded)))
    pieces.update(far)
    distance = ranks // 4
    while distance:
        pieces.update({at ^ distance: hop(x, "head", distance) for at, x in list(pieces.items())})
        distance //= 2
    keys = list(range(ranks))

    block = ((mine, 2 * rows, LANES), BF16)
    all_blocks = pltpu.VMEM((local,) + block[0], BF16)
    back_blocks = pltpu.VMEM((local, mine, packed, LANES), BF16)
    slots = call(
        partial(project_kernel, hd, local, len(keys)),
        "project",
        [block] * local,
        [loaded[4]] + [pieces[at] for at in keys[1:]] + loaded[:4],
        scratch=[all_blocks],
    )
    sketch, first = lax.optimization_barrier((sketch, slots[0]))
    slots = exchange([first, *slots[1:]])
    base, base_after, wb, ba, bb = call(
        partial(prepare_kernel, sk),
        "prepare",
        [((mine, LANES, lanes), F32)] * 2 + [((4 * hd, 4 * LANES), BF16)] + [((4 * LANES, 2 * hd), BF16)] * 2,
        [sketch.transpose(0, 2, 1), prefix_norm, d_norm_end, table],
        [state_t, dstate_t],
        scratch=[
            pltpu.VMEM((2, heads, lanes), F32),
            pltpu.VMEM((mine, hd, feat), F32),
            pltpu.VMEM((mine, hd, feat), F32),
            pltpu.SemaphoreType.DMA((2,)),
        ],
    )

    small = ((mine, window_rows(hd, sk), LANES), BF16)
    qkv, states, key_feats, kdot, total = call(
        partial(key_kernel, sk, hd, local),
        "key_side",
        [
            ((local, mine, 2 * rows, LANES), BF16),
            ((mine, local, LANES, lanes), F32),
            ((mine, local, rows, lanes), BF16),
            ((mine, local, rows, LANES), BF16),
            small,
        ],
        [*slots, wb],
    )

    carry = []
    for d in range(1, groups):
        carry.append(lax.ppermute(total, "group", [(i, i + d) for i in range(groups - d)]))
    carry = carry[:1] if len(carry) < 2 else [sum(x.astype(F32) for x in carry).astype(BF16)]
    side = partial(query_kernel, sk, hd) if carry else partial(query_kernel, sk, hd, None)
    whole = ((mine, local, rows, LANES), F32)
    parts = ((mine, local, rows, 4 * LANES), F32)
    qdot, query_parts, query_feats, dots, near = call(
        partial(query_first_kernel, sk, hd),
        "query_first",
        [
            ((mine, local, rows, LANES), BF16),
            parts,
            ((mine, local, rows, lanes), BF16),
            ((mine, local, rows, rows), F32),
            whole,
        ],
        [qkv, kdot, wb],
    )
    dq, dn, cots, window = call(
        side,
        "query_side",
        [
            ((mine, local, half, LANES), BF16),
            ((mine, local, rows, LANES), BF16),
            ((mine, local, LANES, lanes), F32),
            small,
        ],
        [*carry, base, qkv, kdot, states, query_parts, query_feats, dots, near, ba, bb],
    )

    others = [lax.ppermute(window, "group", [(i, (i + d) % groups) for i in range(groups)]) for d in range(1, groups)]
    key_parts, key_near, dv = call(
        partial(reverse_first_kernel, sk, hd),
        "key_first",
        [parts, whole, whole],
        [qkv, kdot, qdot, dn, wb],
    )
    *gradients, window = call(
        partial(reverse_kernel, sk, hd, len(others)),
        "key_gradients",
        [((mine, packed, LANES), BF16)] * local + [small],
        [window, qkv, dq, key_feats, dn, cots, base_after, key_parts, key_near, dv, bb, *others],
        scratch=[back_blocks],
    )
    gradients = exchange(gradients)

    window, gradients = lax.optimization_barrier((window, gradients))
    spread = exchange([window] * local)

    order = sorted(range(ranks), key=lambda at: [-(at >> bit & 1) for bit in range(ranks.bit_length() - 1)])
    d_query, d_key, d_value, sums, again = call(
        partial(input_kernel, hd, local, order[: ranks // 2]),
        "input_gradient",
        [((rows, width), BF16)] * 3 + [((ranks // 2, rows, depth), BF16), ((3, rows, width), BF16)],
        [*gradients, w_query, w_key, w_value],
        scratch=[back_blocks],
    )
    came = hop(sums, "head", 1)
    (sums,) = call(
        partial(rest_kernel, order[ranks // 2 :]),
        "input_gradient_rest",
        [((ranks // 2, rows, depth), BF16)],
        [again, w_query, w_key, w_value],
    )
    sums = (sums.astype(F32) + came.astype(F32)).astype(BF16)
    distance = 2
    while distance < ranks:
        count = sums.shape[0] // 2
        came = hop(sums[:count], "head", distance)
        sums = (sums[count:].astype(F32) + came.astype(F32)).astype(BF16)
        distance *= 2

    state_out, d_prefix_norm = call(
        partial(expand_kernel, hd, sk, local),
        "prefix_gradients",
        [((heads, hd, feat), F32), ((heads, feat), F32)],
        [*spread, dstate_t, d_norm_end, table],
        scratch=[pltpu.VMEM((heads, hd + 16, lanes), BF16)],
    )
    d_prefix_state = state_out.transpose(0, 2, 1)
    return sums[0], d_query, d_key, d_value, d_prefix_state, d_prefix_norm


def solution(mesh):
    seq, head = mesh.shape["seq"], mesh.shape["head"]

    def run(*args):
        heads = args[5].shape[0] // head
        local = math.gcd(heads, seq)
        local = min(local & -local, GROUP)
        groups = seq // local
        inner = Mesh(mesh.devices.reshape(groups, local, head), ("group", "local", "head"))
        tokens = ("group", "local")
        return jax.shard_map(
            partial(body, groups, local),
            mesh=inner,
            in_specs=(
                P(tokens, "head"),
                P(None, "head"),
                P(None, "head"),
                P(None, "head"),
                P(),
                P("head", None, None),
                P("head", None),
                P(tokens, "head"),
                P("head", None, None),
                P("head", None),
            ),
            out_specs=(
                P(tokens, "head"),
                P(tokens, "head"),
                P(tokens, "head"),
                P(tokens, "head"),
                P("head", None, None),
                P("head", None),
            ),
            check_vma=False,
        )(*args)

    return run
```
